512 devices in a mesh: pts: 256 (over x, z, y), rhs: 2 (over core).
Axes of the slice: x: 4, y: 8, z: 8, core: 2. Of those that a mesh axis runs over, the one named last changes fastest.
Arguments:
- points: bfloat16 [524288, 64], P('pts'), may hold values from -6 to 6
- inputs: bfloat16 [524288, 128], P('pts', 'rhs'), may hold values from -6 to 6
- cotangent: bfloat16 [524288, 128], P('pts', 'rhs'), may hold values from -6 to 6
- order: int32 [524288], P('pts'), may hold values from 0 to 524287, as said below
- near_ids: int32 [2048, 12], P('pts'), may hold values from 0 to 2047, as said below
- near_valid: int32 [2048, 12], P('pts'), may hold values from 0 to 1, as said below
- leaf_basis: bfloat16 [2048, 256, 128], P('pts'), may hold values from -0.375 to 0.375
- local_transfer: bfloat16 [1792, 256, 128], P('pts'), may hold values from -0.375 to 0.375
- chain_transfer: bfloat16 [256, 4, 256, 128], P('pts'), as said below
- leaf_skel: bfloat16 [2048, 128, 64], P('pts'), may hold values from -4 to 4
- local_skel: bfloat16 [1792, 128, 64], P('pts'), may hold values from -4 to 4
- chain_skel: bfloat16 [256, 4, 2, 128, 64], P('pts'), may hold values from -4 to 4, as said below
- top_skel: bfloat16 [16, 128, 64], replicated, may hold values from -4 to 4
Outputs:
- output: bfloat16 [524288, 128], P('pts', 'rhs')
- basis_grad: bfloat16 [2048, 256, 128], P('pts', 'rhs')
The draws below stay inside these ranges and needn't reach their ends.
Inputs may be any that keep to these rules, and one draw needn't show every extreme that they name: `order`: within each aligned block of 2048 rows, a permutation of that block's row indices. `near_ids`: each entry names a leaf of the same aligned block of 8 leaves or of one of the two blocks beside it; slot 0 is the leaf itself; the other slots of a row are distinct and name neither the leaf itself nor its tree sibling. `near_valid`: slot 0 is 1 for every leaf. `chain_transfer`: for each b, the same matrix in every row d with equal d >> (b + 1). chain_skel[d, b, m] equals the skeleton of the same node wherever that node appears, in local_skel and top_skel too.
All inputs are finite; a program needn't handle non-finite values.
Results may differ from the reference program's by a relative error of at most 0.0049.
Values may be sent and summed in bfloat16 or wider, within the bound.
No kernel may reach another device: no remote copies, remote signals or barrier semaphores. Data moves between devices by JAX's collectives and lax.ppermute only.
A program may use at most 64 MiB of HBM per device.

```python
import jax
import jax.numpy as jnp
import numpy as np
from jax import lax

DIM = 64
LEAF = 256
RANK = 128
NB = 12
UP = 4
LEAVES_DEV = 8
NLEAF = 2048
NPTS = 524288
RHS = 128
GROUPS = 16
N_PTS = 256


def skeleton_block(key, span_size, node_index):
    node_key = jax.random.fold_in(jax.random.fold_in(key, span_size), node_index)
    return jax.random.truncated_normal(node_key, -4.0, 4.0, (RANK, DIM), jnp.float32)


def skeleton_many(key, span_table, index_table):
    spans = jnp.asarray(np.asarray(span_table, np.int32).reshape(-1))
    indices = jnp.asarray(np.asarray(index_table, np.int32).reshape(-1))
    blocks = jax.vmap(lambda span_one, index_one: skeleton_block(key, span_one, index_one))(spans, indices)
    return blocks.astype(jnp.bfloat16)


def draw_leaf_skel(key, part):
    return skeleton_many(key, np.ones(NLEAF, np.int32), np.arange(NLEAF))


def draw_local_skel(key, part):
    device_total = NLEAF // LEAVES_DEV
    span_list = []
    offset_list = []
    node_count = LEAVES_DEV // 2
    span_size = 2
    while node_count >= 1:
        span_list = span_list + [span_size] * node_count
        offset_list = offset_list + list(range(node_count))
        node_count = node_count // 2
        span_size = span_size * 2
    span_table = np.array(span_list, np.int32)
    offset_table = np.array(offset_list, np.int32)
    device_ids = np.arange(device_total, dtype=np.int32)[:, None]
    index_table = device_ids * (LEAVES_DEV // span_table)[None, :] + offset_table[None, :]
    span_full = np.broadcast_to(span_table[None, :], index_table.shape)
    return skeleton_many(key, span_full, index_table)


def draw_chain_skel(key, part):
    device_total = NLEAF // LEAVES_DEV
    device_ids = np.arange(device_total, dtype=np.int32)[:, None, None]
    level_ids = np.arange(UP, dtype=np.int32)[None, :, None]
    member_ids = np.arange(2, dtype=np.int32)[None, None, :]
    index_table = (device_ids >> level_ids + 1) * 2 + member_ids
    span_table = np.broadcast_to(LEAVES_DEV * 2 ** level_ids, index_table.shape)
    blocks = skeleton_many(key, span_table, index_table)
    return blocks.reshape(device_total, UP, 2, RANK, DIM)


def draw_top_skel(key, part):
    span_table = np.full(GROUPS, LEAVES_DEV * 2 ** UP, np.int32)
    return skeleton_many(key, span_table, np.arange(GROUPS))


def draw_chain_transfer(key, part):
    key = jax.random.fold_in(key, 11)
    device_total = NLEAF // LEAVES_DEV
    level_ids = np.arange(UP, dtype=np.int32)[None, :]
    parents = np.arange(device_total, dtype=np.int32)[:, None] >> level_ids + 1
    level_full = np.broadcast_to(level_ids, parents.shape)

    def one_parent(level_one, parent_one):
        parent_key = jax.random.fold_in(jax.random.fold_in(key, level_one), parent_one)
        sample = jax.random.truncated_normal(parent_key, -4.0, 4.0, (2 * RANK, RANK), jnp.float32)
        return sample * (1.0 / np.sqrt(2.0 * RANK))
    matrices = jax.vmap(one_parent)(jnp.asarray(level_full.reshape(-1)), jnp.asarray(parents.reshape(-1)))
    return matrices.reshape(device_total, UP, 2 * RANK, RANK).astype(jnp.bfloat16)


def draw_near_ids(key, part):
    key = jax.random.fold_in(key, 21)
    window = 3 * LEAVES_DEV
    leaf_ids = jnp.arange(NLEAF, dtype=jnp.int32)[:, None]
    device_ids = leaf_ids // LEAVES_DEV
    offsets = jnp.arange(window, dtype=jnp.int32)[None, :]
    candidates = (device_ids - 1) * LEAVES_DEV + offsets
    allowed = (candidates >= 0) & (candidates < NLEAF) & (candidates != leaf_ids) & (candidates != jnp.bitwise_xor(leaf_ids, 1))
    raw_draw = jax.random.randint(key, (NLEAF, window), 0, 1 << 16, dtype=jnp.int32)
    scores = jnp.where(allowed, raw_draw * (4 * window) + offsets, -1)
    picked_scores, picked = lax_top(scores, NB - 1)
    chosen = jnp.take_along_axis(candidates, picked, axis=1)
    return jnp.concatenate([leaf_ids, chosen], 1).astype(jnp.int32)


def lax_top(scores, count):
    return jax.lax.top_k(scores, count)


def draw_near_valid(key, part):
    key = jax.random.fold_in(key, 22)
    level_key, slot_key = jax.random.split(key)
    device_total = NLEAF // LEAVES_DEV
    level_draw = jax.random.randint(level_key, (device_total,), 1, 5, dtype=jnp.int32)
    level_draw = jnp.where(jnp.arange(device_total) == 0, 4, level_draw)
    draws = jax.random.randint(slot_key, (NLEAF, NB), 0, 4, dtype=jnp.int32)
    leaf_level = jnp.repeat(level_draw, LEAVES_DEV)[:, None]
    slot_ids = jnp.arange(NB, dtype=jnp.int32)[None, :]
    return jnp.where((draws < leaf_level) | (slot_ids == 0), 1, 0).astype(jnp.int32)


def draw_order(key, part):
    key = jax.random.fold_in(key, 23)
    device_total = NLEAF // LEAVES_DEV
    block_rows = LEAVES_DEV * LEAF
    shuffled = jax.vmap(lambda device_one: jax.random.permutation(jax.random.fold_in(key, device_one), block_rows))(jnp.arange(device_total))
    starts = jnp.arange(device_total, dtype=jnp.int32)[:, None] * block_rows
    return (shuffled.astype(jnp.int32) + starts).reshape(-1).astype(jnp.int32)


def block_scale(rng, extent, cuts, low, top_value):
    gain, own = 1.0, jax.random.fold_in(rng, 6)
    for axis_at, blocks in cuts:
        steps = jnp.exp(jax.random.uniform(jax.random.fold_in(own, axis_at), (blocks,), jnp.float32, low / len(cuts), top_value / len(cuts)))
        gain = gain * jnp.repeat(steps, extent[axis_at] // blocks).reshape([-1 if axis == axis_at else 1 for axis in range(len(extent))])
    return gain


def scatter_about(rng, extent, deviation, limit, shards=(), kind=jnp.bfloat16):
    values = deviation * jax.random.normal(rng, extent, jnp.float32)
    if shards:
        values = values * block_scale(rng, extent, shards, -0.22, 0.18)
    return jnp.clip(values, -limit, limit).astype(kind)


def setup_inputs(seed: int = 0) -> dict:
    arg_keys = jax.random.split(jax.random.key(seed), 14)
    points = scatter_about(arg_keys[0], (NPTS, DIM), 1.0, 6.0, ((0, 256),))
    inputs = scatter_about(arg_keys[1], (NPTS, RHS), 1.0, 6.0, ((0, 256), (1, 2)))
    cotangent = scatter_about(arg_keys[2], (NPTS, RHS), 1.0, 6.0, ((0, 256), (1, 2)))
    order = draw_order(jax.random.fold_in(arg_keys[13], 71), 0)
    near_ids = draw_near_ids(jax.random.fold_in(arg_keys[13], 71), 0)
    near_valid = draw_near_valid(jax.random.fold_in(arg_keys[13], 71), 0)
    leaf_basis = scatter_about(arg_keys[6], (NLEAF, LEAF, RANK), LEAF ** -0.5, 0.375, ((0, 256),))
    local_transfer = scatter_about(arg_keys[7], ((LEAVES_DEV - 1) * N_PTS, 2 * RANK, RANK), (2 * RANK) ** -0.5, 0.375, ((0, 256),))
    chain_transfer = draw_chain_transfer(jax.random.fold_in(arg_keys[13], 71), 0)
    leaf_skel = draw_leaf_skel(jax.random.fold_in(arg_keys[13], 71), 0)
    local_skel = draw_local_skel(jax.random.fold_in(arg_keys[13], 71), 0)
    chain_skel = draw_chain_skel(jax.random.fold_in(arg_keys[13], 71), 0)
    top_skel = draw_top_skel(jax.random.fold_in(arg_keys[13], 71), 0)
    return {"points": points, "inputs": inputs, "cotangent": cotangent, "order": order, "near_ids": near_ids, "near_valid": near_valid, "leaf_basis": leaf_basis, "local_transfer": local_transfer, "chain_transfer": chain_transfer, "leaf_skel": leaf_skel, "local_skel": local_skel, "chain_skel": chain_skel, "top_skel": top_skel}


HIGHEST = lax.Precision.HIGHEST


def kernel_block(left_pts, right_pts):
    left_wide = left_pts.astype(jnp.float32)
    right_wide = right_pts.astype(jnp.float32)
    inner_sum = jnp.einsum('nid,njd->nij', left_pts, right_pts, preferred_element_type=jnp.float32)
    distance = jnp.sum(left_wide * left_wide, -1)[:, :, None] + jnp.sum(right_wide * right_wide, -1)[:, None, :] - 2.0 * inner_sum
    return jnp.exp(distance * (-2.0 / left_pts.shape[-1]))


def sibling_terms(skeletons, coeffs):
    kernel = kernel_block(skeletons[0::2], skeletons[1::2])
    even_term = jnp.einsum('nij,njc->nic', kernel, coeffs[1::2], precision=HIGHEST)
    odd_term = jnp.einsum('nji,njc->nic', kernel, coeffs[0::2], precision=HIGHEST)
    return jnp.stack([even_term, odd_term], 1).reshape(coeffs.shape)


def near_terms(pts_leaf, vals_leaf, near_ids, near_valid):
    def single(item_tuple):
        own_pts, leaf_ids, leaf_valid = item_tuple
        other_pts = jnp.take(pts_leaf, leaf_ids, axis=0)
        other_vals = jnp.take(vals_leaf, leaf_ids, axis=0)
        own_many = jnp.broadcast_to(own_pts, other_pts.shape)
        tile_block = kernel_block(own_many, other_pts) * leaf_valid.astype(jnp.float32)[:, None, None]
        tile_block = tile_block.astype(jnp.bfloat16)
        return jnp.einsum('kab,kbc->ac', tile_block, other_vals, preferred_element_type=jnp.float32)
    return lax.map(single, (pts_leaf, near_ids, near_valid))


def tree_pass(values_leaf, leaf_basis, local_transfer, chain_transfer, leaf_skel, local_skel, chain_skel, top_skel):
    columns = values_leaf.shape[-1]
    coeffs = jnp.einsum('lpr,lpc->lrc', leaf_basis, values_leaf, preferred_element_type=jnp.float32)
    local_count = LEAVES_DEV.bit_length() - 1
    local_mats = local_transfer.reshape(N_PTS, LEAVES_DEV - 1, 2 * RANK, RANK).astype(jnp.float32)
    local_points = local_skel.reshape(N_PTS, LEAVES_DEV - 1, RANK, DIM)
    couplings = []
    transfers = []
    skeletons = leaf_skel
    offset = 0
    node_count = LEAVES_DEV
    for level_index in range(local_count):
        couplings.append(sibling_terms(skeletons, coeffs))
        node_count = node_count // 2
        matrix = local_mats[:, offset:offset + node_count].reshape(-1, 2 * RANK, RANK)
        skeletons = local_points[:, offset:offset + node_count].reshape(-1, RANK, DIM)
        offset = offset + node_count
        coeffs = jnp.einsum('nkr,nkc->nrc', matrix, coeffs.reshape(-1, 2 * RANK, columns), precision=HIGHEST)
        transfers.append(matrix)
    for bit_index in range(UP):
        stride = 2 ** (bit_index + 1)
        skeletons = chain_skel[::stride, bit_index].reshape(-1, RANK, DIM)
        couplings.append(sibling_terms(skeletons, coeffs))
        matrix = chain_transfer[::stride, bit_index].astype(jnp.float32)
        coeffs = jnp.einsum('nkr,nkc->nrc', matrix, coeffs.reshape(-1, 2 * RANK, columns), precision=HIGHEST)
        transfers.append(matrix)
    flat_coeffs = coeffs.reshape(GROUPS * RANK, columns)
    flat_points = top_skel.reshape(1, GROUPS * RANK, DIM)
    kernel = kernel_block(flat_points, flat_points)[0]
    owners = jnp.arange(GROUPS * RANK) // RANK
    kernel = jnp.where(owners[:, None] == owners[None, :], jnp.float32(0.0), kernel)
    field_now = jnp.dot(kernel, flat_coeffs, precision=HIGHEST).reshape(GROUPS, RANK, columns)
    for level_index in reversed(range(local_count + UP)):
        spread = jnp.einsum('nkr,nrc->nkc', transfers[level_index], field_now, precision=HIGHEST)
        field_now = couplings[level_index] + spread.reshape(-1, RANK, columns)
    return field_now


def reference(points, inputs, cotangent, order, near_ids, near_valid, leaf_basis, local_transfer, chain_transfer, leaf_skel, local_skel, chain_skel, top_skel):
    pts_leaf = jnp.take(points, order, axis=0).reshape(NLEAF, LEAF, DIM)
    inputs_leaf = jnp.take(inputs, order, axis=0).reshape(NLEAF, LEAF, RHS)
    cot_leaf = cotangent.reshape(NLEAF, LEAF, RHS)
    near_sum = near_terms(pts_leaf, inputs_leaf, near_ids, near_valid)
    fields = tree_pass(jnp.concatenate([inputs_leaf, cot_leaf], 2), leaf_basis, local_transfer, chain_transfer, leaf_skel, local_skel, chain_skel, top_skel)
    field_in = fields[:, :, :RHS]
    field_cot = fields[:, :, RHS:]
    basis_wide = leaf_basis.astype(jnp.float32)
    output = near_sum + jnp.einsum('lpr,lrc->lpc', basis_wide, field_in, precision=HIGHEST)
    basis_grad = jnp.einsum('lpc,lrc->lpr', cot_leaf.astype(jnp.float32), field_in, precision=HIGHEST)
    basis_grad = basis_grad + jnp.einsum('lpc,lrc->lpr', inputs_leaf.astype(jnp.float32), field_cot, precision=HIGHEST)
    return output.reshape(NPTS, RHS).astype(jnp.bfloat16), basis_grad.astype(jnp.bfloat16)
```

```python
import functools
import math

import jax
import jax.numpy as jnp
from jax import lax
from jax.experimental import pallas as pl
from jax.experimental.pallas import tpu as pltpu
from jax.sharding import PartitionSpec as P

F32 = jnp.float32
BF16 = jnp.bfloat16

LEVELS = 4
MEMBERS = 16
GROUPS = 16
SLAB = 48
SHARE = 8
LEAVES = 8
ROWS = 256
RANK = 128
DIM = 64
SLOTS = 12

VMEM = pl.BlockSpec(memory_space=pltpu.VMEM)
SMEM = pl.BlockSpec(memory_space=pltpu.SMEM)
NN = (((1,), (0,)), ((), ()))
NT = (((1,), (1,)), ((), ()))


def mm(a, b, dims=NN):
    return lax.dot_general(a, b, dims, preferred_element_type=F32)


def split(a):
    high = a.astype(BF16)
    return high, (a - high.astype(F32)).astype(BF16)


def mm2(a, b, dims=NN):
    high, low = split(a)
    return mm(high, b, dims) + mm(low, b, dims)


def lanes(rows, width=128):
    return lax.broadcasted_iota(jnp.int32, (rows, width), 1)


def norm_terms(wide):
    half = -0.5 * jnp.sum(wide * wide, axis=1, keepdims=True)
    first = half.astype(BF16).astype(F32)
    rest = half - first
    second = rest.astype(BF16).astype(F32)
    third = (rest - second).astype(BF16).astype(F32)
    return first, second, third


def extended(pts, base, left, right):
    first, second, third = norm_terms(pts)
    lane = lanes(pts.shape[0], pts.shape[1])
    out = []
    for want, lo, hi in ((left, 0, 3), (right, 3, 0)):
        if not want:
            continue
        value = pts
        for offset, term in ((lo, first), (lo + 1, second), (lo + 2, third)):
            value = jnp.where(lane == base + offset, term, value)
        ones = (lane >= base + hi) & (lane < base + hi + 3)
        out.append(jnp.where(ones, 1.0, value).astype(BF16))
    return out


EXPO = 4.0 / (DIM * math.log(2.0))


def skel_rows(pts):
    wide = pts.astype(F32)
    return jnp.concatenate([wide, jnp.zeros_like(wide)], axis=1)


def kappa(left_pts, right_pts):
    (left,) = extended(skel_rows(left_pts), DIM, True, False)
    (right,) = extended(skel_rows(right_pts), DIM, False, True)
    return jnp.exp2(mm(left, right, NT) * EXPO)


def call(kernel, outs, specs, scratch=(), cost=(0, 0, 0)):
    return pl.pallas_call(
        kernel,
        out_shape=outs,
        in_specs=specs,
        out_specs=jax.tree.map(lambda _: VMEM, outs),
        scratch_shapes=list(scratch),
        compiler_params=pltpu.CompilerParams(vmem_limit_bytes=40 * 2**20),
        cost_estimate=pl.CostEstimate(
            flops=cost[0], bytes_accessed=cost[1], transcendentals=cost[2]
        ),
    )


def sds(shape, dtype):
    return jax.ShapeDtypeStruct(shape, dtype)


def order_kernel(pos, points, inputs, order, joined, source):
    base = pos[0] * (LEAVES * ROWS)
    source[...] = jnp.concatenate([inputs[...], points[...]], axis=1)
    lane = lanes(ROWS).astype(F32).astype(BF16)
    for leaf in range(LEAVES):
        row = order[pl.ds(leaf, 1), :] - base
        low = jnp.bitwise_and(row, 127).astype(F32)
        high = jnp.right_shift(row, 7).astype(F32)
        low = jnp.broadcast_to(low, (128, ROWS)).T.astype(BF16)
        high = jnp.broadcast_to(high, (128, ROWS)).T.astype(BF16)
        one, zero = jnp.ones((), BF16), jnp.zeros((), BF16)
        hit = jnp.where(low == lane, one, zero)
        pick = jnp.concatenate(
            [jnp.where(high == jnp.full((), c, BF16), hit, zero) for c in range(16)], axis=1
        )
        joined[leaf] = mm(pick, source[...]).astype(BF16)


def up_kernel(pos, joined, cot, basis, transfer, chain, both, coeffs, send):
    device = pos[0]
    now = []
    for leaf in range(LEAVES):
        pair = jnp.concatenate(
            [joined[leaf][:, :DIM], cot[leaf]], axis=1
        )
        both[leaf] = pair
        now.append(mm(pair.T, basis[leaf]))
    offset, done = 0, 0
    while len(now) > 1:
        for node, value in enumerate(now):
            coeffs[done + node] = value
        done += len(now)
        now = [
            mm2(jnp.concatenate([now[2 * n], now[2 * n + 1]], axis=1), transfer[offset + n])
            for n in range(len(now) // 2)
        ]
        offset += len(now)
    value = now[0]
    parts = [value]
    for level in range(LEVELS):
        bit = jnp.bitwise_and(jnp.right_shift(device, level), 1)
        half = chain[0, level, pl.ds(pl.multiple_of(bit * RANK, RANK), RANK), :]
        value = mm2(value, half)
        parts.append(value)
    parts = [part.reshape(MEMBERS, SHARE, RANK) for part in parts]
    parts.append(jnp.zeros((MEMBERS, SLAB - 5 * SHARE, RANK), F32))
    send[...] = jnp.concatenate(parts, axis=1).astype(BF16)


def couple_kernel(
    pos, coeffs, leaf_skel, local_skel, chain_skel, top_skel, couplings, chain_k, top_k
):
    device = pos[0]
    group = jnp.right_shift(device, LEVELS)
    for node in range(0, 14, 2):
        if node < 8:
            even, odd = leaf_skel[node], leaf_skel[node + 1]
        else:
            even, odd = local_skel[node - 8], local_skel[node - 7]
        high, low = split(kappa(even, odd))
        for target, other, dims in ((node, node + 1, NT), (node + 1, node, NN)):
            value = coeffs[other]
            couplings[target] = mm2(value, high, dims) + mm(value.astype(BF16), low, dims)
    for level in range(LEVELS):
        bit = jnp.bitwise_and(jnp.right_shift(device, level), 1)
        chain_k[level] = kappa(chain_skel[0, level, 1 - bit], chain_skel[0, level, bit]).astype(BF16)
    mine = top_skel[group]
    for other in range(GROUPS):
        value = kappa(top_skel[other], mine)
        top_k[other] = jnp.where(group == other, 0.0, value).astype(BF16)


def part(received, member, index):
    return received[member].astype(F32)[index * SHARE : (index + 1) * SHARE]


def level_sums(received, index):
    sums = [part(received, member, index) for member in range(MEMBERS)]
    for _ in range(index):
        sums = [sums[2 * n] + sums[2 * n + 1] for n in range(len(sums) // 2)]
    return sums


def total_kernel(received, send):
    total = level_sums(received, LEVELS)[0]
    total = jnp.concatenate([total, jnp.zeros_like(total)], axis=0).astype(BF16)
    for group in range(GROUPS):
        send[group] = total


def reply_kernel(received, totals, top_k, reply):
    flat = jnp.concatenate([totals[group] for group in range(GROUPS)], axis=1)
    field = mm(flat, top_k[...].reshape(GROUPS * RANK, RANK))[:SHARE]
    levels = [level_sums(received, level) for level in range(LEVELS)]
    blank = jnp.zeros((SHARE, RANK), F32)
    for member in range(MEMBERS):
        rows = [levels[level][(member >> level) ^ 1] for level in range(LEVELS)]
        reply[member] = jnp.concatenate(rows + [field, blank], axis=0).astype(BF16)


def down_kernel(pos, replies, chain_k, chain, couplings, transfer, both, fields, give):
    device, core = pos[0], pos[1]
    table = replies[...].astype(F32)
    got = [
        table[:, index * SHARE : (index + 1) * SHARE].reshape(RANK, RANK)
        for index in range(LEVELS + 1)
    ]
    field = got[LEVELS]
    for level in reversed(range(LEVELS)):
        bit = jnp.bitwise_and(jnp.right_shift(device, level), 1)
        half = chain[0, level, pl.ds(pl.multiple_of(bit * RANK, RANK), RANK), :]
        field = mm(got[level].astype(BF16), chain_k[level]) + mm2(field, half, NT)
    now = [field]
    for start, count, offset in ((6, 1, 12), (4, 2, 8), (0, 4, 0)):
        below = []
        for node in range(count):
            spread = mm2(now[node], transfer[start + node], NT)
            for child in range(2):
                rows = spread[:, child * RANK : (child + 1) * RANK]
                below.append(couplings[offset + 2 * node + child] + rows)
        now = below
    away = pl.multiple_of((1 - core) * RANK, RANK)
    for leaf in range(LEAVES):
        fields[leaf] = now[leaf]
        swapped = jnp.concatenate([now[leaf][DIM:], now[leaf][:DIM]], axis=0)
        high, low = split(swapped)
        rows = both[leaf, pl.ds(away, RANK), :]
        give[leaf] = (mm(rows, high) + mm(rows, low)).astype(BF16)


def finish_kernel(pos, fields, both, basis, near, output, keep):
    core = pos[1]
    stay = pl.multiple_of(core * RANK, RANK)
    for leaf in range(LEAVES):
        field = fields[leaf]
        high, low = split(field)
        far = mm(basis[leaf], high, NT) + mm(basis[leaf], low, NT)
        output[pl.ds(leaf * ROWS, ROWS), :] = (near[leaf] + far)[:, :DIM].astype(BF16)
        swapped = jnp.concatenate([field[DIM:], field[:DIM]], axis=0)
        high, low = split(swapped)
        rows = both[leaf, pl.ds(stay, RANK), :]
        keep[leaf] = mm(rows, high) + mm(rows, low)


def prepare_kernel(below, own, above, left, right):
    lane = lanes(ROWS)
    for index, block in enumerate((below, own, above)):
        for leaf in range(LEAVES):
            pts = jnp.where(lane >= DIM, block[leaf].astype(F32), 0.0)
            made = extended(pts, 0, index == 1, True)
            right[index * LEAVES + leaf] = made[-1]
            if index == 1:
                left[leaf] = made[0]


def near_kernel(first, pos, ids, valid, left, right, below, own, above, near, values):
    shift = (pos[0] - 1) * LEAVES
    for index, block in enumerate((below, own, above)):
        values[pl.ds(index * LEAVES, LEAVES)] = block[...]

    def body(step, carry):
        leaf = first + step
        mine = left[leaf]
        total = jnp.zeros((ROWS, 128), F32)
        for slot in range(SLOTS):
            where = ids[leaf, slot] - shift
            used = valid[leaf, slot].astype(F32)
            tile = jnp.exp2(mm(mine, right[where], NT) * EXPO).astype(BF16)
            other = (values[where].astype(F32) * used).astype(BF16)
            total = total + mm(tile, other)
        near[step] = total
        return carry

    lax.fori_loop(0, near.shape[0], body, 0)


def local(
    points,
    inputs,
    cotangent,
    order,
    near_ids,
    near_valid,
    leaf_basis,
    local_transfer,
    chain_transfer,
    leaf_skel,
    local_skel,
    chain_skel,
    top_skel,
):
    device = lax.axis_index("pts")
    core = lax.axis_index("rhs")
    pos = jnp.stack([device, core]).astype(jnp.int32)
    count = lax.axis_size("pts")
    block = (LEAVES, ROWS, 128)

    joined = call(
        order_kernel,
        sds(block, BF16),
        [SMEM, VMEM, VMEM, VMEM],
        [pltpu.VMEM((LEAVES * ROWS, 128), BF16)],
    )(pos, points, inputs, order.reshape(LEAVES, ROWS))

    upward = [(i, i + 1) for i in range(count - 1)]
    below = lax.ppermute(joined, "pts", upward)
    above = lax.ppermute(joined, "pts", [(b, a) for a, b in upward])

    both, coeffs, send = call(
        up_kernel,
        (
            sds(block, BF16),
            sds((14, RANK, RANK), F32),
            sds((MEMBERS, SLAB, RANK), BF16),
        ),
        [SMEM] + [VMEM] * 5,
    )(
        pos,
        joined,
        cotangent.reshape(LEAVES, ROWS, DIM),
        leaf_basis,
        local_transfer,
        chain_transfer,
    )

    groups = [[g * MEMBERS + i for i in range(MEMBERS)] for g in range(GROUPS)]
    across = [[g * MEMBERS + i for g in range(GROUPS)] for i in range(MEMBERS)]
    received = lax.all_to_all(send, "pts", 0, 0, axis_index_groups=groups, tiled=True)

    couplings, chain_k, top_k = call(
        couple_kernel,
        (
            sds((14, RANK, RANK), F32),
            sds((LEVELS, RANK, RANK), BF16),
            sds((GROUPS, RANK, RANK), BF16),
        ),
        [SMEM] + [VMEM] * 5,
        cost=(10**9, 2 * 10**6, 10**6),
    )(pos, coeffs, leaf_skel, local_skel, chain_skel, top_skel)

    left, right = call(
        prepare_kernel,
        (sds(block, BF16), sds((3 * LEAVES, ROWS, 128), BF16)),
        [VMEM] * 3,
        cost=(10**8, 4 * 10**6, 0),
    )(below, joined, above)

    near_parts = []
    per = 4
    for first in range(0, LEAVES, per):
        near_parts.append(
            call(
                functools.partial(near_kernel, first),
                sds((per, ROWS, 128), F32),
                [SMEM, SMEM, SMEM] + [VMEM] * 5,
                [pltpu.VMEM((3 * LEAVES, ROWS, 128), BF16)],
                cost=(per * 4 * 10**8, 4 * 10**6, per * 800000),
            )(pos, near_ids, near_valid, left, right, below, joined, above)
        )
    near = jnp.concatenate(near_parts, axis=0)

    totals = call(
        total_kernel, sds((GROUPS, 2 * SHARE, RANK), BF16), [VMEM]
    )(received)
    totals = lax.all_to_all(totals, "pts", 0, 0, axis_index_groups=across, tiled=True)
    reply = call(
        reply_kernel, sds((MEMBERS, SLAB, RANK), BF16), [VMEM] * 3
    )(received, totals, top_k)
    replies = lax.all_to_all(reply, "pts", 0, 0, axis_index_groups=groups, tiled=True)

    fields, give = call(
        down_kernel,
        (sds((LEAVES, RANK, RANK), F32), sds((LEAVES, RANK, RANK), BF16)),
        [SMEM] + [VMEM] * 6,
    )(pos, replies, chain_k, chain_transfer, couplings, local_transfer, both)
    got = lax.ppermute(give, "rhs", [(0, 1), (1, 0)])
    output, keep = call(
        finish_kernel,
        (sds((LEAVES * ROWS, DIM), BF16), sds((LEAVES, RANK, RANK), F32)),
        [SMEM] + [VMEM] * 4,
        cost=(2 * 10**8, 3 * 10**6, 0),
    )(pos, fields, both, leaf_basis, near)
    basis_grad = (keep + got.astype(F32)).astype(BF16)
    return output, basis_grad


def solution(mesh):
    placed = (
        P("pts", None),
        P("pts", "rhs"),
        P("pts", "rhs"),
        P("pts"),
        P("pts", None),
        P("pts", None),
        P("pts", None, None),
        P("pts", None, None),
        P("pts", None, None, None),
        P("pts", None, None),
        P("pts", None, None),
        P("pts", None, None, None, None),
        P(),
    )
    return jax.shard_map(
        local,
        mesh=mesh,
        in_specs=placed,
        out_specs=(P("pts", "rhs"), P("pts", "rhs", None)),
        check_vma=False,
    )
```

```python
import math

import jax
import jax.numpy as jnp
from jax import lax
from jax.experimental import pallas as pl
from jax.experimental.pallas import tpu as pltpu
from jax.sharding import PartitionSpec as P

F32 = jnp.float32
BF16 = jnp.bfloat16

LEVELS = 4
MEMBERS = 16
GROUPS = 16
SLAB = 48
SHARE = 8
LEAVES = 8
ROWS = 256
RANK = 128
DIM = 64
SLOTS = 12

VMEM = pl.BlockSpec(memory_space=pltpu.VMEM)
ANY = pl.BlockSpec(memory_space=pl.ANY)
HBM = pl.BlockSpec(memory_space=pltpu.HBM)
NN = (((1,), (0,)), ((), ()))
NT = (((1,), (1,)), ((), ()))


def mm(a, b, dims=NN):
    return lax.dot_general(a, b, dims, preferred_element_type=F32)


def split(a):
    high = a.astype(BF16)
    return high, (a - high.astype(F32)).astype(BF16)


def mm2(a, b, dims=NN):
    high, low = split(a)
    return mm(high, b, dims) + mm(low, b, dims)


def lanes(rows, width=128):
    return lax.broadcasted_iota(jnp.int32, (rows, width), 1)


def extended(pts, left, right):
    wide = pts.astype(F32)
    half = -0.5 * jnp.sum(wide * wide, axis=0, keepdims=True)
    first = half.astype(BF16).astype(F32)
    rest = half - first
    second = rest.astype(BF16).astype(F32)
    third = rest - second
    row = lax.broadcasted_iota(jnp.int32, (16, pts.shape[1]), 0)
    out = []
    for want, low, ones in ((left, 0, 3), (right, 3, 0)):
        if not want:
            continue
        value = jnp.where((row >= ones) & (row < ones + 3), 1.0, 0.0)
        for offset, term in enumerate((first, second, third)):
            value = jnp.where(row == low + offset, term, value)
        blank = jnp.zeros((128 - DIM - 16, pts.shape[1]), F32)
        out.append(jnp.concatenate([wide, value, blank], axis=0).astype(BF16))
    return out


EXPO = 4.0 / (DIM * math.log(2.0))


def kappa(left_pts, right_pts):
    (left,) = extended(left_pts, True, False)
    (right,) = extended(right_pts, False, True)
    return jnp.exp2(mm(left.T, right) * EXPO)


def call(kernel, outs, specs, scratch=(), cost=(0, 0, 0), places=None, room=60):
    return pl.pallas_call(
        kernel,
        out_shape=outs,
        in_specs=specs,
        out_specs=places or jax.tree.map(lambda _: VMEM, outs),
        scratch_shapes=list(scratch),
        compiler_params=pltpu.CompilerParams(vmem_limit_bytes=int(room * 2**20)),
        cost_estimate=pl.CostEstimate(
            flops=cost[0], bytes_accessed=cost[1], transcendentals=cost[2]
        ),
    )


def sds(shape, dtype):
    return jax.ShapeDtypeStruct(shape, dtype)


def fetch(pairs, sems):
    copies = [
        pltpu.make_async_copy(source, target, sems.at[index])
        for index, (source, target) in enumerate(pairs)
    ]
    for copy in copies:
        copy.start()
    return [copy.wait for copy in copies]


def rise_kernel(
    points,
    inputs,
    order,
    cot,
    basis,
    transfer,
    chain,
    joined,
    coeffs,
    send,
    raw_v,
    order_v,
    cot_v,
    basis_v,
    transfer_v,
    chain_v,
    joined_v,
    coeffs_v,
    source_v,
    in_sems,
    joined_sems,
    coeff_sems,
):
    waits = fetch(
        (
            (points, raw_v.at[pl.ds(DIM, DIM)]),
            (inputs, raw_v.at[pl.ds(0, DIM)]),
            (order, order_v),
            (cot, cot_v),
            (basis, basis_v),
            (transfer, transfer_v),
            (chain, chain_v),
        ),
        in_sems,
    )
    device = lax.axis_index("pts")
    base = device * (LEAVES * ROWS)
    for wait in waits[:3]:
        wait()
    for index in range(4):
        low = raw_v[:, pl.ds(index * 512, ROWS)].T
        high = raw_v[:, pl.ds(index * 512 + ROWS, ROWS)].T
        source_v[index] = jnp.concatenate([low, high], axis=1)
    lane = lanes(ROWS, ROWS).astype(F32).astype(BF16)
    one, zero = jnp.ones((), BF16), jnp.zeros((), BF16)
    joined_copies = []
    for leaf in range(LEAVES):
        pieces = [order_v[pl.ds(2 * leaf + index, 1), :] - base for index in range(2)]
        row = jnp.concatenate(pieces, axis=1)
        low = jnp.bitwise_and(row, 255).astype(F32)
        high = jnp.right_shift(row, 8).astype(F32)
        low = jnp.broadcast_to(low, (128, ROWS)).T.astype(BF16)
        high = jnp.broadcast_to(high, (128, ROWS)).T
        hit = jnp.where(jnp.concatenate([low, low], axis=1) == lane, one, zero)
        value = jnp.zeros((ROWS, 128), F32)
        for index in range(4):
            found = mm(hit, source_v[index])
            value = jnp.where(high == 2.0 * index, found[:, :128], value)
            value = jnp.where(high == 2.0 * index + 1.0, found[:, 128:], value)
        joined_v[leaf] = value.astype(BF16)
        copy = pltpu.make_async_copy(joined_v.at[leaf], joined.at[leaf], joined_sems.at[leaf])
        copy.start()
        joined_copies.append(copy)
    for wait in waits[3:]:
        wait()
    now = []
    for leaf in range(LEAVES):
        theirs = cot_v[:, pl.ds(leaf * ROWS, ROWS)]
        pair = jnp.concatenate([joined_v[leaf].T[:DIM], theirs], axis=0)
        now.append(mm(pair, basis_v[leaf]))
    offset, done, level = 0, 0, 0
    coeff_copies = []
    while len(now) > 1:
        for node, value in enumerate(now):
            coeffs_v[done + node] = value
        span = pl.ds(done, len(now))
        copy = pltpu.make_async_copy(coeffs_v.at[span], coeffs.at[span], coeff_sems.at[level])
        copy.start()
        coeff_copies.append(copy)
        done += len(now)
        level += 1
        now = [
            mm2(jnp.concatenate([now[2 * n], now[2 * n + 1]], axis=1), transfer_v[offset + n])
            for n in range(len(now) // 2)
        ]
        offset += len(now)
    value = now[0]
    parts = [value]
    for level in range(LEVELS):
        bit = jnp.bitwise_and(jnp.right_shift(device, level), 1)
        half = chain_v[0, level, pl.ds(pl.multiple_of(bit * RANK, RANK), RANK), :]
        value = mm2(value, half)
        parts.append(value)
    parts = [part.reshape(MEMBERS, SHARE, RANK) for part in parts]
    parts.append(jnp.zeros((MEMBERS, SLAB - 5 * SHARE, RANK), F32))
    send[...] = jnp.concatenate(parts, axis=1).astype(BF16)
    for copy in joined_copies + coeff_copies:
        copy.wait()


def couple_kernel(
    coeffs,
    joined,
    cot,
    leaf_skel,
    local_skel,
    chain_skel,
    top_skel,
    after,
    couplings,
    chain_k,
    both,
    top_k,
    coeffs_v,
    joined_v,
    cot_v,
    leaf_v,
    local_v,
    skel_v,
    top_v,
    couplings_v,
    chain_k_v,
    both_v,
    sems,
    out_sems,
):
    waits = fetch(
        (
            (cot, cot_v),
            (joined, joined_v),
            (chain_skel, skel_v),
            (leaf_skel, leaf_v),
            (local_skel, local_v),
            (coeffs, coeffs_v),
            (top_skel, top_v),
        ),
        sems,
    )
    device = lax.axis_index("pts")
    for wait in waits[:3]:
        wait()
    for leaf in range(LEAVES):
        theirs = cot_v[:, pl.ds(leaf * ROWS, ROWS)].T
        both_v[leaf] = jnp.concatenate([joined_v[leaf][:, :DIM], theirs], axis=1)
    done = fetch(((both_v, both),), out_sems)
    for level in range(LEVELS):
        bit = jnp.bitwise_and(jnp.right_shift(device, level), 1)
        chain_k_v[level] = kappa(skel_v[0, level, 1 - bit], skel_v[0, level, bit]).astype(BF16)
    done += fetch(((chain_k_v, chain_k),), out_sems.at[pl.ds(1, 1)])
    for wait in waits[3:6]:
        wait()
    for node in range(0, 14, 2):
        if node < 8:
            even, odd = leaf_v[node], leaf_v[node + 1]
        else:
            even, odd = local_v[node - 8], local_v[node - 7]
        high, low = split(kappa(even, odd))
        for target, other, dims in ((node, node + 1, NT), (node + 1, node, NN)):
            value = coeffs_v[other]
            couplings_v[target] = mm2(value, high, dims) + mm(value.astype(BF16), low, dims)
    done += fetch(((couplings_v, couplings),), out_sems.at[pl.ds(2, 1)])
    waits[6]()
    group = jnp.right_shift(device, LEVELS)
    mine = top_v[group]
    for other in range(GROUPS):
        value = kappa(top_v[other], mine)
        top_k[other] = jnp.where(group == other, 0.0, value).astype(BF16)
    for wait in done:
        wait()


def part(received, member, index):
    return received[member].astype(F32)[index * SHARE : (index + 1) * SHARE]


def level_sums(received, index):
    sums = [part(received, member, index) for member in range(MEMBERS)]
    for _ in range(index):
        sums = [sums[2 * n] + sums[2 * n + 1] for n in range(len(sums) // 2)]
    return sums


def total_kernel(received, send):
    total = level_sums(received, LEVELS)[0]
    total = jnp.concatenate([total, jnp.zeros_like(total)], axis=0).astype(BF16)
    for group in range(GROUPS):
        send[group] = total


def reply_kernel(received, totals, top_k, reply):
    flat = jnp.concatenate([totals[group] for group in range(GROUPS)], axis=1)
    field = mm(flat, top_k[...].reshape(GROUPS * RANK, RANK))[:SHARE]
    levels = [level_sums(received, level) for level in range(LEVELS)]
    blank = jnp.zeros((SHARE, RANK), F32)
    for member in range(MEMBERS):
        rows = [levels[level][(member >> level) ^ 1] for level in range(LEVELS)]
        reply[member] = jnp.concatenate(rows + [field, blank], axis=0).astype(BF16)


def down_kernel(
    replies,
    chain_k,
    chain,
    transfer,
    couplings,
    both,
    basis,
    near,
    give,
    output,
    keep,
    replies_v,
    chain_k_v,
    chain_v,
    transfer_v,
    couplings_v,
    both_v,
    basis_v,
    near_v,
    give_v,
    output_v,
    keep_v,
    sems,
    out_sems,
):
    waits = fetch(
        (
            (replies, replies_v),
            (chain_k, chain_k_v),
            (chain, chain_v),
            (transfer, transfer_v),
            (couplings, couplings_v),
            (both, both_v),
            (basis, basis_v),
            (near, near_v),
        ),
        sems,
    )
    device, core = lax.axis_index("pts"), lax.axis_index("rhs")
    for wait in waits[:3]:
        wait()
    table = replies_v[...].astype(F32)
    got = [
        table[:, index * SHARE : (index + 1) * SHARE].reshape(RANK, RANK)
        for index in range(LEVELS + 1)
    ]
    field = got[LEVELS]
    for level in reversed(range(LEVELS)):
        bit = jnp.bitwise_and(jnp.right_shift(device, level), 1)
        half = chain_v[0, level, pl.ds(pl.multiple_of(bit * RANK, RANK), RANK), :]
        field = mm(got[level].astype(BF16), chain_k_v[level]) + mm2(field, half, NT)
    waits[3]()
    waits[4]()
    now = [field]
    for start, count, offset in ((6, 1, 12), (4, 2, 8), (0, 4, 0)):
        below = []
        for node in range(count):
            spread = mm2(now[node], transfer_v[start + node], NT)
            for child in range(2):
                rows = spread[:, child * RANK : (child + 1) * RANK]
                below.append(couplings_v[offset + 2 * node + child] + rows)
        now = below
    for wait in waits[5:]:
        wait()
    away = pl.multiple_of((1 - core) * RANK, RANK)
    stay = pl.multiple_of(core * RANK, RANK)
    for leaf in range(LEAVES):
        swapped = jnp.concatenate([now[leaf][DIM:], now[leaf][:DIM]], axis=0)
        high, low = split(swapped)
        for target, first in ((give_v, away), (keep_v, stay)):
            rows = both_v[leaf, pl.ds(first, RANK), :]
            target[leaf] = (mm(rows, high) + mm(rows, low)).astype(target.dtype)
    done = fetch(((give_v, give), (keep_v, keep)), out_sems)
    for leaf in range(LEAVES):
        high, low = split(now[leaf])
        far = mm(basis_v[leaf], high, NT) + mm(basis_v[leaf], low, NT)
        total = (near_v[leaf] + far).astype(BF16)
        output_v[:, pl.ds(leaf * ROWS, ROWS)] = total.T[:DIM]
    done += fetch(((output_v, output),), out_sems.at[pl.ds(2, 1)])
    for wait in done:
        wait()


def near_kernel(
    ids,
    valid,
    below,
    own,
    above,
    after,
    near,
    ids_v,
    valid_v,
    below_v,
    above_v,
    own_v,
    left,
    right,
    values,
    near_v,
    sems,
    near_sems,
):
    waits = fetch(
        (
            (below, below_v),
            (own, own_v),
            (above, above_v),
            (ids, ids_v),
            (valid, valid_v),
        ),
        sems,
    )
    for index, block in enumerate((below_v, own_v, above_v)):
        waits[index]()
        for leaf in range(LEAVES):
            value = block[leaf]
            made = extended(value.T[DIM:], index == 1, True)
            right[index * LEAVES + leaf] = made[-1]
            values[index * LEAVES + leaf] = value
            if index == 1:
                left[leaf] = made[0].T
    device = lax.axis_index("pts")
    shift = (device - 1) * LEAVES

    def body(leaf, carry):
        mine = left[leaf]
        total = jnp.zeros((ROWS, 128), F32)
        for slot in range(SLOTS):
            where = ids_v[leaf, slot] - shift
            used = jnp.full((1, 128), valid_v[leaf, slot], jnp.int32).astype(F32).astype(BF16)
            tile = jnp.exp2(mm(mine, right[where]) * EXPO).astype(BF16)
            total = total + mm(tile, values[where] * used)
        near_v[leaf] = total
        pltpu.make_async_copy(near_v.at[leaf], near.at[leaf], near_sems.at[leaf]).start()
        return carry

    waits[3]()
    waits[4]()
    lax.fori_loop(0, LEAVES, body, 0)
    for leaf in range(LEAVES):
        pltpu.make_async_copy(near_v.at[leaf], near.at[leaf], near_sems.at[leaf]).wait()


def local(
    points,
    inputs,
    cotangent,
    order,
    near_ids,
    near_valid,
    leaf_basis,
    local_transfer,
    chain_transfer,
    leaf_skel,
    local_skel,
    chain_skel,
    top_skel,
):
    count = lax.axis_size("pts")
    block = (LEAVES, ROWS, 128)

    points, inputs, cot = points.T, inputs.T, cotangent.T
    leaf_skel, local_skel, chain_skel, top_skel = (
        jnp.swapaxes(skel, -1, -2) for skel in (leaf_skel, local_skel, chain_skel, top_skel)
    )
    order = order.reshape(2 * LEAVES, 128)
    joined, coeffs, send = call(
        rise_kernel,
        (
            sds(block, BF16),
            sds((14, RANK, RANK), F32),
            sds((MEMBERS, SLAB, RANK), BF16),
        ),
        [HBM] * 7,
        [
            pltpu.VMEM((2 * DIM, LEAVES * ROWS), BF16),
            pltpu.VMEM((2 * LEAVES, 128), jnp.int32),
            pltpu.VMEM((DIM, LEAVES * ROWS), BF16),
            pltpu.VMEM(block, BF16),
            pltpu.VMEM(local_transfer.shape, BF16),
            pltpu.VMEM(chain_transfer.shape, BF16),
            pltpu.VMEM(block, BF16),
            pltpu.VMEM((14, RANK, RANK), F32),
            pltpu.VMEM((4, ROWS, 256), BF16),
            pltpu.SemaphoreType.DMA((7,)),
            pltpu.SemaphoreType.DMA((LEAVES,)),
            pltpu.SemaphoreType.DMA((3,)),
        ],
        places=(HBM, HBM, VMEM),
    )(points, inputs, order, cot, leaf_basis, local_transfer, chain_transfer)

    groups = [[g * MEMBERS + i for i in range(MEMBERS)] for g in range(GROUPS)]
    across = [[g * MEMBERS + i for g in range(GROUPS)] for i in range(MEMBERS)]
    received = lax.all_to_all(send, "pts", 0, 0, axis_index_groups=groups, tiled=True)

    upward = [(i, i + 1) for i in range(count - 1)]
    below = lax.ppermute(joined, "pts", upward)
    above = lax.ppermute(joined, "pts", [(b, a) for a, b in upward])

    total = call(
        total_kernel, sds((GROUPS, 2 * SHARE, RANK), BF16), [VMEM], room=8
    )(received)
    totals = lax.all_to_all(total, "pts", 0, 0, axis_index_groups=across, tiled=True)

    tree = (14, RANK, RANK)
    square = (LEAVES, RANK, RANK)
    links = (LEVELS, RANK, RANK)
    couplings, chain_k, both, top_k = call(
        couple_kernel,
        (sds(tree, F32), sds(links, BF16), sds(block, BF16), sds((GROUPS, RANK, RANK), BF16)),
        [HBM] * 7 + [ANY],
        [
            pltpu.VMEM(tree, F32),
            pltpu.VMEM(block, BF16),
            pltpu.VMEM((DIM, LEAVES * ROWS), BF16),
            pltpu.VMEM(leaf_skel.shape, BF16),
            pltpu.VMEM(local_skel.shape, BF16),
            pltpu.VMEM(chain_skel.shape, BF16),
            pltpu.VMEM(top_skel.shape, BF16),
            pltpu.VMEM(tree, F32),
            pltpu.VMEM(links, BF16),
            pltpu.VMEM(block, BF16),
            pltpu.SemaphoreType.DMA((7,)),
            pltpu.SemaphoreType.DMA((3,)),
        ],
        cost=(2 * 10**9, 4 * 10**6, 10**6),
        places=(HBM, HBM, HBM, VMEM),
    )(coeffs, joined, cot, leaf_skel, local_skel, chain_skel, top_skel, total)

    reply = call(
        reply_kernel, sds((MEMBERS, SLAB, RANK), BF16), [VMEM] * 3, room=8
    )(received, totals, top_k)
    replies = lax.all_to_all(reply, "pts", 0, 0, axis_index_groups=groups, tiled=True)

    near = call(
        near_kernel,
        sds((LEAVES, ROWS, 128), F32),
        [HBM] * 5 + [ANY],
        [
            pltpu.SMEM((LEAVES, SLOTS), jnp.int32),
            pltpu.SMEM((LEAVES, SLOTS), jnp.int32),
            pltpu.VMEM(block, BF16),
            pltpu.VMEM(block, BF16),
            pltpu.VMEM(block, BF16),
            pltpu.VMEM(block, BF16),
            pltpu.VMEM((3 * LEAVES, 128, ROWS), BF16),
            pltpu.VMEM((3 * LEAVES, ROWS, 128), BF16),
            pltpu.VMEM((LEAVES, ROWS, 128), F32),
            pltpu.SemaphoreType.DMA((5,)),
            pltpu.SemaphoreType.DMA((LEAVES,)),
        ],
        cost=(LEAVES * 4 * 10**8, 4 * 10**6, LEAVES * 800000),
        places=HBM,
        room=60,
    )(near_ids, near_valid, below, joined, above, reply)

    give, output, keep = call(
        down_kernel,
        (sds(square, BF16), sds((DIM, LEAVES * ROWS), BF16), sds(square, F32)),
        [HBM] * 8,
        [
            pltpu.VMEM((MEMBERS, SLAB, RANK), BF16),
            pltpu.VMEM(links, BF16),
            pltpu.VMEM(chain_transfer.shape, BF16),
            pltpu.VMEM(local_transfer.shape, BF16),
            pltpu.VMEM(tree, F32),
            pltpu.VMEM(block, BF16),
            pltpu.VMEM(block, BF16),
            pltpu.VMEM(block, F32),
            pltpu.VMEM(square, BF16),
            pltpu.VMEM((DIM, LEAVES * ROWS), BF16),
            pltpu.VMEM(square, F32),
            pltpu.SemaphoreType.DMA((8,)),
            pltpu.SemaphoreType.DMA((3,)),
        ],
        places=(HBM,) * 3,
        room=60,
    )(
        replies,
        chain_k,
        chain_transfer,
        local_transfer,
        couplings,
        both,
        leaf_basis,
        near,
    )
    got = lax.ppermute(give, "rhs", [(0, 1), (1, 0)])
    basis_grad = (keep + got.astype(F32)).astype(BF16)
    return output.T, basis_grad


def solution(mesh):
    placed = (
        P("pts", None),
        P("pts", "rhs"),
        P("pts", "rhs"),
        P("pts"),
        P("pts", None),
        P("pts", None),
        P("pts", None, None),
        P("pts", None, None),
        P("pts", None, None, None),
        P("pts", None, None),
        P("pts", None, None),
        P("pts", None, None, None, None),
        P(),
    )
    return jax.shard_map(
        local,
        mesh=mesh,
        in_specs=placed,
        out_specs=(P("pts", "rhs"), P("pts", "rhs", None)),
        check_vma=False,
    )
```

```python
import math

import jax
import jax.numpy as jnp
from jax import lax
from jax.experimental import pallas as pl
from jax.experimental.pallas import tpu as pltpu
from jax.sharding import PartitionSpec as P

F32 = jnp.float32
BF16 = jnp.bfloat16

LEVELS = 4
MEMBERS = 16
GROUPS = 16
SLAB = 48
SHARE = 8
LEAVES = 8
ROWS = 256
RANK = 128
DIM = 64
SLOTS = 12

VMEM = pl.BlockSpec(memory_space=pltpu.VMEM)
ANY = pl.BlockSpec(memory_space=pl.ANY)
HBM = pl.BlockSpec(memory_space=pltpu.HBM)
NN = (((1,), (0,)), ((), ()))
NT = (((1,), (1,)), ((), ()))


def mm(a, b, dims=NN):
    return lax.dot_general(a, b, dims, preferred_element_type=F32)


def split(a):
    high = a.astype(BF16)
    return high, (a - high.astype(F32)).astype(BF16)


def mm2(a, b, dims=NN):
    high, low = split(a)
    along = dims[0][1][0]
    return mm(jnp.concatenate([high, low], axis=1), jnp.concatenate([b, b], axis=along), dims)


def lanes(rows, width=128):
    return lax.broadcasted_iota(jnp.int32, (rows, width), 1)


def norm_rows(pts, left, right):
    wide = pts.astype(F32)
    half = -0.5 * jnp.sum(wide * wide, axis=0, keepdims=True)
    first = half.astype(BF16).astype(F32)
    rest = half - first
    second = rest.astype(BF16).astype(F32)
    third = rest - second
    row = lax.broadcasted_iota(jnp.int32, (16, pts.shape[1]), 0)
    out = []
    for want, low, ones in ((left, 0, 3), (right, 3, 0)):
        if not want:
            continue
        value = jnp.where((row >= ones) & (row < ones + 3), 1.0, 0.0)
        for offset, term in enumerate((first, second, third)):
            value = jnp.where(row == low + offset, term, value)
        out.append(value)
    return out


def extended(pts, left, right):
    blank = jnp.zeros((128 - DIM - 16, pts.shape[1]), BF16)
    return [
        jnp.concatenate([pts, rows.astype(BF16), blank], axis=0)
        for rows in norm_rows(pts, left, right)
    ]


EXPO = 4.0 / (DIM * math.log(2.0))


def kappa(left_pts, right_pts):
    (left,) = extended(left_pts, True, False)
    (right,) = extended(right_pts, False, True)
    return jnp.exp2(mm(left.T, right) * EXPO)


def call(kernel, outs, specs, scratch=(), cost=(0, 0, 0), places=None, room=60):
    return pl.pallas_call(
        kernel,
        out_shape=outs,
        in_specs=specs,
        out_specs=places or jax.tree.map(lambda _: VMEM, outs),
        scratch_shapes=list(scratch),
        compiler_params=pltpu.CompilerParams(vmem_limit_bytes=int(room * 2**20)),
        cost_estimate=pl.CostEstimate(
            flops=cost[0], bytes_accessed=cost[1], transcendentals=cost[2]
        ),
    )


def sds(shape, dtype):
    return jax.ShapeDtypeStruct(shape, dtype)


def fetch(pairs, sems):
    copies = [
        pltpu.make_async_copy(source, target, sems.at[index])
        for index, (source, target) in enumerate(pairs)
    ]
    for copy in copies:
        copy.start()
    return [copy.wait for copy in copies]


def rise_kernel(
    points,
    inputs,
    order,
    cot,
    basis,
    transfer,
    chain,
    joined,
    coeffs,
    send,
    raw_v,
    order_v,
    cot_v,
    basis_v,
    transfer_v,
    chain_v,
    joined_v,
    coeffs_v,
    source_v,
    in_sems,
    joined_sems,
    coeff_sems,
):
    waits = fetch(
        (
            (points, raw_v.at[pl.ds(DIM, DIM)]),
            (inputs, raw_v.at[pl.ds(0, DIM)]),
            (order, order_v),
            (cot, cot_v),
            (basis, basis_v),
            (transfer, transfer_v),
            (chain, chain_v),
        ),
        in_sems,
    )
    device = lax.axis_index("pts")
    base = device * (LEAVES * ROWS)
    for wait in waits[:3]:
        wait()
    for index in range(4):
        low = raw_v[:, pl.ds(index * 512, ROWS)].T
        high = raw_v[:, pl.ds(index * 512 + ROWS, ROWS)].T
        source_v[index] = jnp.concatenate([low, high], axis=1)
    lane = lanes(ROWS, ROWS).astype(F32).astype(BF16)
    one, zero = jnp.ones((), BF16), jnp.zeros((), BF16)
    joined_copies = []
    for leaf in range(LEAVES):
        pieces = [order_v[pl.ds(2 * leaf + index, 1), :] - base for index in range(2)]
        row = jnp.concatenate(pieces, axis=1)
        low = jnp.bitwise_and(row, 255).astype(F32)
        high = jnp.right_shift(row, 8).astype(F32)
        low = jnp.broadcast_to(low, (128, ROWS)).T.astype(BF16)
        high = jnp.broadcast_to(high, (128, ROWS)).T
        hit = jnp.where(jnp.concatenate([low, low], axis=1) == lane, one, zero)
        value = jnp.zeros((ROWS, 128), F32)
        for index in range(4):
            found = mm(hit, source_v[index])
            value = jnp.where(high == 2.0 * index, found[:, :128], value)
            value = jnp.where(high == 2.0 * index + 1.0, found[:, 128:], value)
        joined_v[leaf] = value.astype(BF16)
        copy = pltpu.make_async_copy(joined_v.at[leaf], joined.at[leaf], joined_sems.at[leaf])
        copy.start()
        joined_copies.append(copy)
    for wait in waits[3:]:
        wait()
    now = []
    for leaf in range(LEAVES):
        theirs = cot_v[:, pl.ds(leaf * ROWS, ROWS)]
        pair = jnp.concatenate([joined_v[leaf].T[:DIM], theirs], axis=0)
        now.append(mm(pair, basis_v[leaf]))
    offset, done, level = 0, 0, 0
    coeff_copies = []
    while len(now) > 1:
        for node, value in enumerate(now):
            coeffs_v[done + node] = value
        span = pl.ds(done, len(now))
        copy = pltpu.make_async_copy(coeffs_v.at[span], coeffs.at[span], coeff_sems.at[level])
        copy.start()
        coeff_copies.append(copy)
        done += len(now)
        level += 1
        now = [
            mm2(jnp.concatenate([now[2 * n], now[2 * n + 1]], axis=1), transfer_v[offset + n])
            for n in range(len(now) // 2)
        ]
        offset += len(now)
    value = now[0]
    parts = [value]
    for level in range(LEVELS):
        bit = jnp.bitwise_and(jnp.right_shift(device, level), 1)
        half = chain_v[0, level, pl.ds(pl.multiple_of(bit * RANK, RANK), RANK), :]
        value = mm(value.astype(BF16), half)
        parts.append(value)
    parts = [part.reshape(MEMBERS, SHARE, RANK) for part in parts]
    parts.append(jnp.zeros((MEMBERS, SLAB - 5 * SHARE, RANK), F32))
    send[...] = jnp.concatenate(parts, axis=1).astype(BF16)
    for copy in joined_copies + coeff_copies:
        copy.wait()


def couple_kernel(
    coeffs,
    joined,
    cot,
    leaf_skel,
    local_skel,
    chain_skel,
    after,
    couplings,
    chain_k,
    both,
    coeffs_v,
    joined_v,
    cot_v,
    leaf_v,
    local_v,
    skel_v,
    couplings_v,
    chain_k_v,
    both_v,
    sems,
    out_sems,
):
    waits = fetch(
        (
            (cot, cot_v),
            (joined, joined_v),
            (chain_skel, skel_v),
            (leaf_skel, leaf_v),
            (local_skel, local_v),
            (coeffs, coeffs_v),
        ),
        sems,
    )
    device = lax.axis_index("pts")
    for wait in waits[:3]:
        wait()
    for leaf in range(LEAVES):
        theirs = cot_v[:, pl.ds(leaf * ROWS, ROWS)].T
        both_v[leaf] = jnp.concatenate([joined_v[leaf][:, :DIM], theirs], axis=1)
    done = fetch(((both_v, both),), out_sems)
    for level in range(LEVELS):
        bit = jnp.bitwise_and(jnp.right_shift(device, level), 1)
        chain_k_v[level] = kappa(skel_v[0, level, 1 - bit], skel_v[0, level, bit]).astype(BF16)
    done += fetch(((chain_k_v, chain_k),), out_sems.at[pl.ds(1, 1)])
    for wait in waits[3:6]:
        wait()
    for node in range(0, 14, 2):
        if node < 8:
            even, odd = leaf_v[node], leaf_v[node + 1]
        else:
            even, odd = local_v[node - 8], local_v[node - 7]
        near_k = kappa(even, odd).astype(BF16)
        for target, other, dims in ((node, node + 1, NT), (node + 1, node, NN)):
            couplings_v[target] = mm2(coeffs_v[other], near_k, dims)
    done += fetch(((couplings_v, couplings),), out_sems.at[pl.ds(2, 1)])
    for wait in done:
        wait()


def part(received, member, index):
    return received[member].astype(F32)[index * SHARE : (index + 1) * SHARE]


def level_sums(received, index):
    sums = [part(received, member, index) for member in range(MEMBERS)]
    for _ in range(index):
        sums = [sums[2 * n] + sums[2 * n + 1] for n in range(len(sums) // 2)]
    return sums


def total_kernel(received, send):
    total = level_sums(received, LEVELS)[0]
    total = jnp.concatenate([total, jnp.zeros_like(total)], axis=0).astype(BF16)
    for group in range(GROUPS):
        send[group] = total


def reply_kernel(received, totals, top_skel, reply):
    flat = jnp.concatenate([totals[group] for group in range(GROUPS)], axis=1)
    group = jnp.right_shift(lax.axis_index("pts"), LEVELS)
    (mine,) = extended(top_skel[group], False, True)
    top_k = []
    for other in range(GROUPS):
        (theirs,) = extended(top_skel[other], True, False)
        value = jnp.exp2(mm(theirs.T, mine) * EXPO)
        top_k.append(jnp.where(group == other, 0.0, value).astype(BF16))
    field = mm(flat, jnp.concatenate(top_k, axis=0))[:SHARE]
    levels = [level_sums(received, level) for level in range(LEVELS)]
    blank = jnp.zeros((SHARE, RANK), F32)
    for member in range(MEMBERS):
        rows = [levels[level][(member >> level) ^ 1] for level in range(LEVELS)]
        reply[member] = jnp.concatenate(rows + [field, blank], axis=0).astype(BF16)


def down_kernel(
    replies,
    chain_k,
    chain,
    transfer,
    couplings,
    both,
    basis,
    near,
    give,
    output,
    keep,
    replies_v,
    chain_k_v,
    chain_v,
    transfer_v,
    couplings_v,
    both_v,
    basis_v,
    near_v,
    give_v,
    output_v,
    keep_v,
    sems,
    out_sems,
):
    waits = fetch(
        (
            (replies, replies_v),
            (chain_k, chain_k_v),
            (chain, chain_v),
            (transfer, transfer_v),
            (couplings, couplings_v),
            (both, both_v),
            (basis, basis_v),
            (near, near_v),
        ),
        sems,
    )
    device, core = lax.axis_index("pts"), lax.axis_index("rhs")
    for wait in waits[:3]:
        wait()
    table = replies_v[...].astype(F32)
    got = [
        table[:, index * SHARE : (index + 1) * SHARE].reshape(RANK, RANK)
        for index in range(LEVELS + 1)
    ]
    field = got[LEVELS]
    for level in reversed(range(LEVELS)):
        bit = jnp.bitwise_and(jnp.right_shift(device, level), 1)
        half = chain_v[0, level, pl.ds(pl.multiple_of(bit * RANK, RANK), RANK), :]
        field = mm(got[level].astype(BF16), chain_k_v[level]) + mm(field.astype(BF16), half, NT)
    waits[3]()
    waits[4]()
    now = [field]
    for start, count, offset in ((6, 1, 12), (4, 2, 8), (0, 4, 0)):
        below = []
        for node in range(count):
            spread = mm2(now[node], transfer_v[start + node], NT)
            for child in range(2):
                rows = spread[:, child * RANK : (child + 1) * RANK]
                below.append(couplings_v[offset + 2 * node + child] + rows)
        now = below
    for wait in waits[5:]:
        wait()
    away = pl.multiple_of((1 - core) * RANK, RANK)
    stay = pl.multiple_of(core * RANK, RANK)
    for leaf in range(LEAVES):
        swapped = jnp.concatenate([now[leaf][DIM:], now[leaf][:DIM]], axis=0)
        terms = jnp.concatenate(split(swapped), axis=0)
        for target, first in ((give_v, away), (keep_v, stay)):
            rows = both_v[leaf, pl.ds(first, RANK), :]
            target[leaf] = mm(jnp.concatenate([rows, rows], axis=1), terms).astype(BF16)
    done = fetch(((give_v, give), (keep_v, keep)), out_sems)
    for leaf in range(LEAVES):
        far = mm(now[leaf][:DIM].astype(BF16), basis_v[leaf], NT)
        output_v[:, pl.ds(leaf * ROWS, ROWS)] = (near_v[leaf] + far).astype(BF16)
    done += fetch(((output_v, output),), out_sems.at[pl.ds(2, 1)])
    for wait in done:
        wait()


def near_kernel(
    ids,
    valid,
    below,
    own,
    above,
    after,
    near,
    ids_v,
    valid_v,
    own_v,
    left,
    right,
    values,
    near_v,
    sems,
    near_sems,
):
    waits = fetch(((own, own_v), (ids, ids_v), (valid, valid_v)), sems)
    lane = lanes(ROWS)
    for index, block in ((0, below), (2, above), (1, own_v)):
        if index == 1:
            waits[0]()
        for leaf in range(LEAVES):
            value = block[leaf]
            turned = value.T
            made = norm_rows(turned[DIM:], index == 1, True)
            spare = jnp.concatenate([made[-1].T, jnp.zeros((ROWS, 112), F32)], axis=1)
            values[index * LEAVES + leaf] = turned[:DIM]
            right[index * LEAVES + leaf] = jnp.where(
                lane < DIM, spare, value.astype(F32)
            ).astype(BF16)
            if index == 1:
                blank = jnp.zeros((DIM - 16, ROWS), BF16)
                left[leaf] = jnp.concatenate(
                    [made[0].astype(BF16), blank, turned[DIM:]], axis=0
                )
    shift = (lax.axis_index("pts") - 1) * LEAVES
    waits[1]()
    waits[2]()

    def body(leaf, carry):
        mine = left[leaf]
        total = jnp.zeros((DIM, ROWS), F32)
        for start in range(0, SLOTS, 4):
            tiles, others = [], []
            for slot in range(start, start + 4):
                where = ids_v[leaf, slot] - shift
                used = jnp.full((1, ROWS), valid_v[leaf, slot], jnp.int32).astype(F32).astype(BF16)
                tiles.append(jnp.exp2(mm(right[where], mine) * EXPO).astype(BF16))
                others.append(values[where] * used)
            total = total + mm(jnp.concatenate(others, axis=1), jnp.concatenate(tiles, axis=0))
        near_v[leaf] = total
        pltpu.make_async_copy(near_v.at[leaf], near.at[leaf], near_sems.at[leaf]).start()
        return carry

    lax.fori_loop(0, LEAVES, body, 0)
    for leaf in range(LEAVES):
        pltpu.make_async_copy(near_v.at[leaf], near.at[leaf], near_sems.at[leaf]).wait()


def local(
    points,
    inputs,
    cotangent,
    order,
    near_ids,
    near_valid,
    leaf_basis,
    local_transfer,
    chain_transfer,
    leaf_skel,
    local_skel,
    chain_skel,
    top_skel,
):
    count = lax.axis_size("pts")
    block = (LEAVES, ROWS, 128)

    points, inputs, cot = points.T, inputs.T, cotangent.T
    leaf_skel, local_skel, chain_skel, top_skel = (
        jnp.swapaxes(skel, -1, -2) for skel in (leaf_skel, local_skel, chain_skel, top_skel)
    )
    order = order.reshape(2 * LEAVES, 128)
    joined, coeffs, send = call(
        rise_kernel,
        (
            sds(block, BF16),
            sds((14, RANK, RANK), F32),
            sds((MEMBERS, SLAB, RANK), BF16),
        ),
        [HBM] * 7,
        [
            pltpu.VMEM((2 * DIM, LEAVES * ROWS), BF16),
            pltpu.VMEM((2 * LEAVES, 128), jnp.int32),
            pltpu.VMEM((DIM, LEAVES * ROWS), BF16),
            pltpu.VMEM(block, BF16),
            pltpu.VMEM(local_transfer.shape, BF16),
            pltpu.VMEM(chain_transfer.shape, BF16),
            pltpu.VMEM(block, BF16),
            pltpu.VMEM((14, RANK, RANK), F32),
            pltpu.VMEM((4, ROWS, 256), BF16),
            pltpu.SemaphoreType.DMA((7,)),
            pltpu.SemaphoreType.DMA((LEAVES,)),
            pltpu.SemaphoreType.DMA((3,)),
        ],
        places=(HBM, HBM, VMEM),
    )(points, inputs, order, cot, leaf_basis, local_transfer, chain_transfer)

    groups = [[g * MEMBERS + i for i in range(MEMBERS)] for g in range(GROUPS)]
    across = [[g * MEMBERS + i for g in range(GROUPS)] for i in range(MEMBERS)]
    received = lax.all_to_all(send, "pts", 0, 0, axis_index_groups=groups, tiled=True)

    upward = [(i, i + 1) for i in range(count - 1)]
    below = lax.ppermute(joined, "pts", upward)
    above = lax.ppermute(joined, "pts", [(b, a) for a, b in upward])

    total = call(
        total_kernel, sds((GROUPS, 2 * SHARE, RANK), BF16), [VMEM], room=8
    )(received)
    totals = lax.all_to_all(total, "pts", 0, 0, axis_index_groups=across, tiled=True)

    tree = (14, RANK, RANK)
    square = (LEAVES, RANK, RANK)
    links = (LEVELS, RANK, RANK)
    couplings, chain_k, both = call(
        couple_kernel,
        (sds(tree, F32), sds(links, BF16), sds(block, BF16)),
        [HBM] * 6 + [ANY],
        [
            pltpu.VMEM(tree, F32),
            pltpu.VMEM(block, BF16),
            pltpu.VMEM((DIM, LEAVES * ROWS), BF16),
            pltpu.VMEM(leaf_skel.shape, BF16),
            pltpu.VMEM(local_skel.shape, BF16),
            pltpu.VMEM(chain_skel.shape, BF16),
            pltpu.VMEM(tree, F32),
            pltpu.VMEM(links, BF16),
            pltpu.VMEM(block, BF16),
            pltpu.SemaphoreType.DMA((6,)),
            pltpu.SemaphoreType.DMA((3,)),
        ],
        cost=(2 * 10**9, 4 * 10**6, 10**6),
        places=(HBM,) * 3,
    )(coeffs, joined, cot, leaf_skel, local_skel, chain_skel, total)

    reply = call(
        reply_kernel, sds((MEMBERS, SLAB, RANK), BF16), [VMEM] * 3, room=8
    )(received, totals, top_skel)
    replies = lax.all_to_all(reply, "pts", 0, 0, axis_index_groups=groups, tiled=True)

    near = call(
        near_kernel,
        sds((LEAVES, DIM, ROWS), F32),
        [HBM, HBM, VMEM, HBM, VMEM, ANY],
        [
            pltpu.SMEM((LEAVES, SLOTS), jnp.int32),
            pltpu.SMEM((LEAVES, SLOTS), jnp.int32),
            pltpu.VMEM(block, BF16),
            pltpu.VMEM((LEAVES, 128, ROWS), BF16),
            pltpu.VMEM((3 * LEAVES, ROWS, 128), BF16),
            pltpu.VMEM((3 * LEAVES, DIM, ROWS), BF16),
            pltpu.VMEM((LEAVES, DIM, ROWS), F32),
            pltpu.SemaphoreType.DMA((3,)),
            pltpu.SemaphoreType.DMA((LEAVES,)),
        ],
        cost=(5 * 10**10, 4 * 10**6, LEAVES * 800000),
        places=HBM,
        room=14,
    )(near_ids, near_valid, below, joined, above, reply)

    give, output, keep = call(
        down_kernel,
        (sds(square, BF16), sds((DIM, LEAVES * ROWS), BF16), sds(square, BF16)),
        [HBM] * 8,
        [
            pltpu.VMEM((MEMBERS, SLAB, RANK), BF16),
            pltpu.VMEM(links, BF16),
            pltpu.VMEM(chain_transfer.shape, BF16),
            pltpu.VMEM(local_transfer.shape, BF16),
            pltpu.VMEM(tree, F32),
            pltpu.VMEM(block, BF16),
            pltpu.VMEM(block, BF16),
            pltpu.VMEM((LEAVES, DIM, ROWS), F32),
            pltpu.VMEM(square, BF16),
            pltpu.VMEM((DIM, LEAVES * ROWS), BF16),
            pltpu.VMEM(square, BF16),
            pltpu.SemaphoreType.DMA((8,)),
            pltpu.SemaphoreType.DMA((3,)),
        ],
        places=(HBM,) * 3,
        room=60,
    )(
        replies,
        chain_k,
        chain_transfer,
        local_transfer,
        couplings,
        both,
        leaf_basis,
        near,
    )
    got = lax.ppermute(give, "rhs", [(0, 1), (1, 0)])
    basis_grad = (keep.astype(F32) + got.astype(F32)).astype(BF16)
    return output.T, basis_grad


def solution(mesh):
    placed = (
        P("pts", None),
        P("pts", "rhs"),
        P("pts", "rhs"),
        P("pts"),
        P("pts", None),
        P("pts", None),
        P("pts", None, None),
        P("pts", None, None),
        P("pts", None, None, None),
        P("pts", None, None),
        P("pts", None, None),
        P("pts", None, None, None, None),
        P(),
    )
    return jax.shard_map(
        local,
        mesh=mesh,
        in_specs=placed,
        out_specs=(P("pts", "rhs"), P("pts", "rhs", None)),
        check_vma=False,
    )
```

```python
import math

import jax
import jax.numpy as jnp
from jax import lax
from jax.experimental import pallas as pl
from jax.experimental.pallas import tpu as pltpu
from jax.sharding import PartitionSpec as P

F32 = jnp.float32
BF16 = jnp.bfloat16

LEVELS = 4
MEMBERS = 16
GROUPS = 16
SLAB = 48
SHARE = 8
LEAVES = 8
ROWS = 256
RANK = 128
DIM = 64
SLOTS = 12

VMEM = pl.BlockSpec(memory_space=pltpu.VMEM)
ANY = pl.BlockSpec(memory_space=pl.ANY)
HBM = pl.BlockSpec(memory_space=pltpu.HBM)
NN = (((1,), (0,)), ((), ()))
NT = (((1,), (1,)), ((), ()))


def mm(a, b, dims=NN):
    return lax.dot_general(a, b, dims, preferred_element_type=F32)


def split(a):
    high = a.astype(BF16)
    return high, (a - high.astype(F32)).astype(BF16)


def mm2(a, b, dims=NN):
    high, low = split(a)
    along = dims[0][1][0]
    return mm(jnp.concatenate([high, low], axis=1), jnp.concatenate([b, b], axis=along), dims)


def lanes(rows, width=128):
    return lax.broadcasted_iota(jnp.int32, (rows, width), 1)


def norm_rows(pts, left, right):
    wide = pts.astype(F32)
    half = -0.5 * jnp.sum(wide * wide, axis=0, keepdims=True)
    first = half.astype(BF16).astype(F32)
    rest = half - first
    second = rest.astype(BF16).astype(F32)
    third = rest - second
    row = lax.broadcasted_iota(jnp.int32, (16, pts.shape[1]), 0)
    out = []
    for want, low, ones in ((left, 0, 3), (right, 3, 0)):
        if not want:
            continue
        value = jnp.where((row >= ones) & (row < ones + 3), 1.0, 0.0)
        for offset, term in enumerate((first, second, third)):
            value = jnp.where(row == low + offset, term, value)
        out.append(value)
    return out


def extended(pts, left, right):
    blank = jnp.zeros((128 - DIM - 16, pts.shape[1]), BF16)
    return [
        jnp.concatenate([pts, rows.astype(BF16), blank], axis=0)
        for rows in norm_rows(pts, left, right)
    ]


EXPO = 4.0 / (DIM * math.log(2.0))


def kappa(left_pts, right_pts):
    (left,) = extended(left_pts, True, False)
    (right,) = extended(right_pts, False, True)
    return jnp.exp2(mm(left.T, right) * EXPO)


def call(kernel, outs, specs, scratch=(), cost=(0, 0, 0), places=None, room=60):
    return pl.pallas_call(
        kernel,
        out_shape=outs,
        in_specs=specs,
        out_specs=places or jax.tree.map(lambda _: VMEM, outs),
        scratch_shapes=list(scratch),
        compiler_params=pltpu.CompilerParams(vmem_limit_bytes=int(room * 2**20)),
        cost_estimate=pl.CostEstimate(
            flops=cost[0], bytes_accessed=cost[1], transcendentals=cost[2]
        ),
    )


def sds(shape, dtype):
    return jax.ShapeDtypeStruct(shape, dtype)


def fetch(pairs, sems):
    copies = [
        pltpu.make_async_copy(source, target, sems.at[index])
        for index, (source, target) in enumerate(pairs)
    ]
    for copy in copies:
        copy.start()
    return [copy.wait for copy in copies]


def rise_kernel(
    points,
    inputs,
    order,
    cot,
    basis,
    transfer,
    chain,
    joined,
    coeffs,
    send,
    raw_v,
    order_v,
    cot_v,
    basis_v,
    transfer_v,
    chain_v,
    joined_v,
    coeffs_v,
    source_v,
    in_sems,
    joined_sems,
    coeff_sems,
):
    waits = fetch(
        (
            (points, raw_v.at[pl.ds(DIM, DIM)]),
            (inputs, raw_v.at[pl.ds(0, DIM)]),
            (order, order_v),
            (cot, cot_v),
            (basis, basis_v),
            (transfer, transfer_v),
            (chain, chain_v),
        ),
        in_sems,
    )
    device = lax.axis_index("pts")
    base = device * (LEAVES * ROWS)
    for wait in waits[:3]:
        wait()
    for index in range(4):
        low = raw_v[:, pl.ds(index * 512, ROWS)].T
        high = raw_v[:, pl.ds(index * 512 + ROWS, ROWS)].T
        source_v[index] = jnp.concatenate([low, high], axis=1)
    lane = lanes(ROWS, ROWS).astype(F32).astype(BF16)
    one, zero = jnp.ones((), BF16), jnp.zeros((), BF16)
    joined_copies = []
    for leaf in range(LEAVES):
        pieces = [order_v[pl.ds(2 * leaf + index, 1), :] - base for index in range(2)]
        row = jnp.concatenate(pieces, axis=1)
        low = jnp.bitwise_and(row, 255).astype(F32)
        high = jnp.right_shift(row, 8).astype(F32)
        low = jnp.broadcast_to(low, (128, ROWS)).T.astype(BF16)
        high = jnp.broadcast_to(high, (128, ROWS)).T
        hit = jnp.where(jnp.concatenate([low, low], axis=1) == lane, one, zero)
        value = jnp.zeros((ROWS, 128), F32)
        for index in range(4):
            found = mm(hit, source_v[index])
            value = jnp.where(high == 2.0 * index, found[:, :128], value)
            value = jnp.where(high == 2.0 * index + 1.0, found[:, 128:], value)
        joined_v[leaf] = value.astype(BF16)
        copy = pltpu.make_async_copy(joined_v.at[leaf], joined.at[leaf], joined_sems.at[leaf])
        copy.start()
        joined_copies.append(copy)
    for wait in waits[3:]:
        wait()
    now = []
    for leaf in range(LEAVES):
        theirs = cot_v[:, pl.ds(leaf * ROWS, ROWS)]
        pair = jnp.concatenate([joined_v[leaf].T[:DIM], theirs], axis=0)
        now.append(mm(pair, basis_v[leaf]))
    offset, done, level = 0, 0, 0
    coeff_copies = []
    while len(now) > 1:
        for node, value in enumerate(now):
            coeffs_v[done + node] = value
        span = pl.ds(done, len(now))
        copy = pltpu.make_async_copy(coeffs_v.at[span], coeffs.at[span], coeff_sems.at[level])
        copy.start()
        coeff_copies.append(copy)
        done += len(now)
        level += 1
        now = [
            mm2(jnp.concatenate([now[2 * n], now[2 * n + 1]], axis=1), transfer_v[offset + n])
            for n in range(len(now) // 2)
        ]
        offset += len(now)
    value = now[0]
    parts = [value]
    for level in range(LEVELS):
        bit = jnp.bitwise_and(jnp.right_shift(device, level), 1)
        half = chain_v[0, level, pl.ds(pl.multiple_of(bit * RANK, RANK), RANK), :]
        value = mm(value.astype(BF16), half)
        parts.append(value)
    parts = [part.reshape(MEMBERS, SHARE, RANK) for part in parts]
    parts.append(jnp.zeros((MEMBERS, SLAB - 5 * SHARE, RANK), F32))
    send[...] = jnp.concatenate(parts, axis=1).astype(BF16)
    for copy in joined_copies + coeff_copies:
        copy.wait()


def couple_kernel(
    coeffs,
    joined,
    cot,
    leaf_skel,
    local_skel,
    chain_skel,
    after,
    couplings,
    chain_k,
    both,
    coeffs_v,
    joined_v,
    cot_v,
    leaf_v,
    local_v,
    skel_v,
    couplings_v,
    chain_k_v,
    both_v,
    sems,
    out_sems,
):
    waits = fetch(
        (
            (cot, cot_v),
            (joined, joined_v),
            (chain_skel, skel_v),
            (leaf_skel, leaf_v),
            (local_skel, local_v),
            (coeffs, coeffs_v),
        ),
        sems,
    )
    device = lax.axis_index("pts")
    for wait in waits[:3]:
        wait()
    for leaf in range(LEAVES):
        theirs = cot_v[:, pl.ds(leaf * ROWS, ROWS)].T
        both_v[leaf] = jnp.concatenate([joined_v[leaf][:, :DIM], theirs], axis=1)
    done = fetch(((both_v, both),), out_sems)
    for level in range(LEVELS):
        bit = jnp.bitwise_and(jnp.right_shift(device, level), 1)
        chain_k_v[level] = kappa(skel_v[0, level, 1 - bit], skel_v[0, level, bit]).astype(BF16)
    done += fetch(((chain_k_v, chain_k),), out_sems.at[pl.ds(1, 1)])
    for wait in waits[3:6]:
        wait()
    for node in range(0, 14, 2):
        if node < 8:
            even, odd = leaf_v[node], leaf_v[node + 1]
        else:
            even, odd = local_v[node - 8], local_v[node - 7]
        near_k = kappa(even, odd).astype(BF16)
        for target, other, dims in ((node, node + 1, NT), (node + 1, node, NN)):
            couplings_v[target] = mm2(coeffs_v[other], near_k, dims)
    done += fetch(((couplings_v, couplings),), out_sems.at[pl.ds(2, 1)])
    for wait in done:
        wait()


def part(received, member, index):
    return received[member].astype(F32)[index * SHARE : (index + 1) * SHARE]


def level_sums(received, index):
    sums = [part(received, member, index) for member in range(MEMBERS)]
    for _ in range(index):
        sums = [sums[2 * n] + sums[2 * n + 1] for n in range(len(sums) // 2)]
    return sums


def total_kernel(received, send):
    total = level_sums(received, LEVELS)[0]
    total = jnp.concatenate([total, jnp.zeros_like(total)], axis=0).astype(BF16)
    for group in range(GROUPS):
        send[group] = total


def reply_kernel(received, totals, top_skel, reply):
    flat = jnp.concatenate([totals[group] for group in range(GROUPS)], axis=1)
    group = jnp.right_shift(lax.axis_index("pts"), LEVELS)
    (mine,) = extended(top_skel[group], False, True)
    top_k = []
    for other in range(GROUPS):
        (theirs,) = extended(top_skel[other], True, False)
        value = jnp.exp2(mm(theirs.T, mine) * EXPO)
        top_k.append(jnp.where(group == other, 0.0, value).astype(BF16))
    field = mm(flat, jnp.concatenate(top_k, axis=0))[:SHARE]
    levels = [level_sums(received, level) for level in range(LEVELS)]
    blank = jnp.zeros((SHARE, RANK), F32)
    for member in range(MEMBERS):
        rows = [levels[level][(member >> level) ^ 1] for level in range(LEVELS)]
        reply[member] = jnp.concatenate(rows + [field, blank], axis=0).astype(BF16)


def down_kernel(
    replies, chain_k, chain, transfer, couplings, both, basis, near, give, output, keep
):
    device, core = lax.axis_index("pts"), lax.axis_index("rhs")
    table = replies[...].astype(F32)
    got = [
        table[:, index * SHARE : (index + 1) * SHARE].reshape(RANK, RANK)
        for index in range(LEVELS + 1)
    ]
    field = got[LEVELS]
    for level in reversed(range(LEVELS)):
        bit = jnp.bitwise_and(jnp.right_shift(device, level), 1)
        half = chain[0, level, pl.ds(pl.multiple_of(bit * RANK, RANK), RANK), :]
        field = mm(got[level].astype(BF16), chain_k[level]) + mm(field.astype(BF16), half, NT)
    now = [field]
    for start, count, offset in ((6, 1, 12), (4, 2, 8), (0, 4, 0)):
        below = []
        for node in range(count):
            spread = mm2(now[node], transfer[start + node], NT)
            for child in range(2):
                rows = spread[:, child * RANK : (child + 1) * RANK]
                below.append(couplings[offset + 2 * node + child] + rows)
        now = below
    away = pl.multiple_of((1 - core) * RANK, RANK)
    stay = pl.multiple_of(core * RANK, RANK)
    for leaf in range(LEAVES):
        swapped = jnp.concatenate([now[leaf][DIM:], now[leaf][:DIM]], axis=0)
        terms = jnp.concatenate(split(swapped), axis=0)
        for target, first in ((give, away), (keep, stay)):
            rows = both[leaf, pl.ds(first, RANK), :]
            target[leaf] = mm(jnp.concatenate([rows, rows], axis=1), terms).astype(target.dtype)
    for leaf in range(LEAVES):
        far = mm(now[leaf][:DIM].astype(BF16), basis[leaf], NT)
        output[:, pl.ds(leaf * ROWS, ROWS)] = (near[leaf] + far).astype(BF16)


def near_kernel(
    ids,
    valid,
    swap_a,
    own,
    swap_b,
    after,
    near,
    ids_v,
    valid_v,
    own_v,
    left,
    right,
    values,
    near_v,
    sems,
    near_sems,
):
    waits = fetch(((own, own_v), (ids, ids_v), (valid, valid_v)), sems)
    lane = lanes(ROWS)
    device = lax.axis_index("pts")
    odd = jnp.bitwise_and(device, 1)
    places = ((2 - 2 * odd) * LEAVES, LEAVES, 2 * odd * LEAVES)
    for index, block in ((0, swap_a), (2, swap_b), (1, own_v)):
        if index == 1:
            waits[0]()
        for leaf in range(LEAVES):
            value = block[leaf]
            turned = value.T
            made = norm_rows(turned[DIM:], index == 1, True)
            spare = jnp.concatenate([made[-1].T, jnp.zeros((ROWS, 112), F32)], axis=1)
            values[places[index] + leaf] = turned[:DIM]
            right[places[index] + leaf] = jnp.where(
                lane < DIM, spare, value.astype(F32)
            ).astype(BF16)
            if index == 1:
                blank = jnp.zeros((DIM - 16, ROWS), BF16)
                left[leaf] = jnp.concatenate(
                    [made[0].astype(BF16), blank, turned[DIM:]], axis=0
                )
    shift = (device - 1) * LEAVES
    waits[1]()
    waits[2]()

    def body(leaf, carry):
        mine = left[leaf]
        total = jnp.zeros((DIM, ROWS), F32)
        for start in range(0, SLOTS, 4):
            tiles, others = [], []
            for slot in range(start, start + 4):
                where = ids_v[leaf, slot] - shift
                used = jnp.full((1, ROWS), valid_v[leaf, slot], jnp.int32).astype(F32).astype(BF16)
                tiles.append(jnp.exp2(mm(right[where], mine) * EXPO).astype(BF16))
                others.append(values[where] * used)
            total = total + mm(jnp.concatenate(others, axis=1), jnp.concatenate(tiles, axis=0))
        near_v[leaf] = total
        pltpu.make_async_copy(near_v.at[leaf], near.at[leaf], near_sems.at[leaf]).start()
        return carry

    lax.fori_loop(0, LEAVES, body, 0)
    for leaf in range(LEAVES):
        pltpu.make_async_copy(near_v.at[leaf], near.at[leaf], near_sems.at[leaf]).wait()


def local(
    points,
    inputs,
    cotangent,
    order,
    near_ids,
    near_valid,
    leaf_basis,
    local_transfer,
    chain_transfer,
    leaf_skel,
    local_skel,
    chain_skel,
    top_skel,
):
    count = lax.axis_size("pts")
    block = (LEAVES, ROWS, 128)

    points, inputs, cot = points.T, inputs.T, cotangent.T
    leaf_skel, local_skel, chain_skel, top_skel = (
        jnp.swapaxes(skel, -1, -2) for skel in (leaf_skel, local_skel, chain_skel, top_skel)
    )
    order = order.reshape(2 * LEAVES, 128)
    joined, coeffs, send = call(
        rise_kernel,
        (
            sds(block, BF16),
            sds((14, RANK, RANK), F32),
            sds((MEMBERS, SLAB, RANK), BF16),
        ),
        [HBM] * 7,
        [
            pltpu.VMEM((2 * DIM, LEAVES * ROWS), BF16),
            pltpu.VMEM((2 * LEAVES, 128), jnp.int32),
            pltpu.VMEM((DIM, LEAVES * ROWS), BF16),
            pltpu.VMEM(block, BF16),
            pltpu.VMEM(local_transfer.shape, BF16),
            pltpu.VMEM(chain_transfer.shape, BF16),
            pltpu.VMEM(block, BF16),
            pltpu.VMEM((14, RANK, RANK), F32),
            pltpu.VMEM((4, ROWS, 256), BF16),
            pltpu.SemaphoreType.DMA((7,)),
            pltpu.SemaphoreType.DMA((LEAVES,)),
            pltpu.SemaphoreType.DMA((3,)),
        ],
        places=(HBM, HBM, VMEM),
    )(points, inputs, order, cot, leaf_basis, local_transfer, chain_transfer)

    groups = [[g * MEMBERS + i for i in range(MEMBERS)] for g in range(GROUPS)]
    across = [[g * MEMBERS + i for g in range(GROUPS)] for i in range(MEMBERS)]
    received = lax.all_to_all(send, "pts", 0, 0, axis_index_groups=groups, tiled=True)

    swaps = []
    for first in (0, 1):
        pairs = [(i, i + 1) for i in range(first, count - 1, 2)]
        swaps.append(lax.ppermute(joined, "pts", pairs + [(b, a) for a, b in pairs]))

    total = call(
        total_kernel, sds((GROUPS, 2 * SHARE, RANK), BF16), [VMEM], room=8
    )(received)
    totals = lax.all_to_all(total, "pts", 0, 0, axis_index_groups=across, tiled=True)

    tree = (14, RANK, RANK)
    square = (LEAVES, RANK, RANK)
    links = (LEVELS, RANK, RANK)
    couplings, chain_k, both = call(
        couple_kernel,
        (sds(tree, F32), sds(links, BF16), sds(block, BF16)),
        [HBM] * 6 + [ANY],
        [
            pltpu.VMEM(tree, F32),
            pltpu.VMEM(block, BF16),
            pltpu.VMEM((DIM, LEAVES * ROWS), BF16),
            pltpu.VMEM(leaf_skel.shape, BF16),
            pltpu.VMEM(local_skel.shape, BF16),
            pltpu.VMEM(chain_skel.shape, BF16),
            pltpu.VMEM(tree, F32),
            pltpu.VMEM(links, BF16),
            pltpu.VMEM(block, BF16),
            pltpu.SemaphoreType.DMA((6,)),
            pltpu.SemaphoreType.DMA((3,)),
        ],
        cost=(2 * 10**9, 4 * 10**6, 10**6),
        places=(HBM,) * 3,
    )(coeffs, joined, cot, leaf_skel, local_skel, chain_skel, total)

    reply = call(
        reply_kernel, sds((MEMBERS, SLAB, RANK), BF16), [VMEM] * 3, room=8
    )(received, totals, top_skel)
    replies = lax.all_to_all(reply, "pts", 0, 0, axis_index_groups=groups, tiled=True)

    near = call(
        near_kernel,
        sds((LEAVES, DIM, ROWS), F32),
        [HBM, HBM, VMEM, HBM, VMEM, ANY],
        [
            pltpu.SMEM((LEAVES, SLOTS), jnp.int32),
            pltpu.SMEM((LEAVES, SLOTS), jnp.int32),
            pltpu.VMEM(block, BF16),
            pltpu.VMEM((LEAVES, 128, ROWS), BF16),
            pltpu.VMEM((3 * LEAVES, ROWS, 128), BF16),
            pltpu.VMEM((3 * LEAVES, DIM, ROWS), BF16),
            pltpu.VMEM((LEAVES, DIM, ROWS), F32),
            pltpu.SemaphoreType.DMA((3,)),
            pltpu.SemaphoreType.DMA((LEAVES,)),
        ],
        cost=(5 * 10**10, 4 * 10**6, LEAVES * 800000),
        places=HBM,
        room=14,
    )(near_ids, near_valid, swaps[0], joined, swaps[1], reply)

    give, output, keep = call(
        down_kernel,
        (sds(square, BF16), sds((DIM, LEAVES * ROWS), BF16), sds(square, F32)),
        [VMEM] * 8,
        room=14,
    )(
        replies,
        chain_k,
        chain_transfer,
        local_transfer,
        couplings,
        both,
        leaf_basis,
        near,
    )
    got = lax.ppermute(give, "rhs", [(0, 1), (1, 0)])
    basis_grad = (keep + got.astype(F32)).astype(BF16)
    return output.T, basis_grad


def solution(mesh):
    placed = (
        P("pts", None),
        P("pts", "rhs"),
        P("pts", "rhs"),
        P("pts"),
        P("pts", None),
        P("pts", None),
        P("pts", None, None),
        P("pts", None, None),
        P("pts", None, None, None),
        P("pts", None, None),
        P("pts", None, None),
        P("pts", None, None, None, None),
        P(),
    )
    return jax.shard_map(
        local,
        mesh=mesh,
        in_specs=placed,
        out_specs=(P("pts", "rhs"), P("pts", "rhs", None)),
        check_vma=False,
    )
```

```python
import math

import jax
import jax.numpy as jnp
from jax import lax
from jax.experimental import pallas as pl
from jax.experimental.pallas import tpu as pltpu
from jax.sharding import PartitionSpec as P

F32 = jnp.float32
BF16 = jnp.bfloat16

LEVELS = 4
MEMBERS = 16
GROUPS = 16
SLAB = 48
SHARE = 8
LEAVES = 8
ROWS = 256
RANK = 128
DIM = 64
SLOTS = 12

VMEM = pl.BlockSpec(memory_space=pltpu.VMEM)
ANY = pl.BlockSpec(memory_space=pl.ANY)
HBM = pl.BlockSpec(memory_space=pltpu.HBM)
NN = (((1,), (0,)), ((), ()))
NT = (((1,), (1,)), ((), ()))


def mm(a, b, dims=NN):
    return lax.dot_general(a, b, dims, preferred_element_type=F32)


def split(a):
    high = a.astype(BF16)
    return high, (a - high.astype(F32)).astype(BF16)


def mm2(a, b, dims=NN):
    high, low = split(a)
    along = dims[0][1][0]
    return mm(jnp.concatenate([high, low], axis=1), jnp.concatenate([b, b], axis=along), dims)


def lanes(rows, width=128):
    return lax.broadcasted_iota(jnp.int32, (rows, width), 1)


def norm_rows(pts, left, right):
    wide = pts.astype(F32)
    half = -0.5 * jnp.sum(wide * wide, axis=0, keepdims=True)
    first = half.astype(BF16).astype(F32)
    rest = half - first
    second = rest.astype(BF16).astype(F32)
    third = rest - second
    row = lax.broadcasted_iota(jnp.int32, (16, pts.shape[1]), 0)
    out = []
    for want, low, ones in ((left, 0, 3), (right, 3, 0)):
        if not want:
            continue
        value = jnp.where((row >= ones) & (row < ones + 3), 1.0, 0.0)
        for offset, term in enumerate((first, second, third)):
            value = jnp.where(row == low + offset, term, value)
        out.append(value)
    return out


def extended(pts, left, right):
    blank = jnp.zeros((128 - DIM - 16, pts.shape[1]), BF16)
    return [
        jnp.concatenate([pts, rows.astype(BF16), blank], axis=0)
        for rows in norm_rows(pts, left, right)
    ]


EXPO = 4.0 / (DIM * math.log(2.0))


def kappa(left_pts, right_pts):
    (left,) = extended(left_pts, True, False)
    (right,) = extended(right_pts, False, True)
    return jnp.exp2(mm(left.T, right) * EXPO)


def call(kernel, outs, specs, scratch=(), cost=(0, 0, 0), places=None, room=60):
    return pl.pallas_call(
        kernel,
        out_shape=outs,
        in_specs=specs,
        out_specs=places or jax.tree.map(lambda _: VMEM, outs),
        scratch_shapes=list(scratch),
        compiler_params=pltpu.CompilerParams(vmem_limit_bytes=int(room * 2**20)),
        cost_estimate=pl.CostEstimate(
            flops=cost[0], bytes_accessed=cost[1], transcendentals=cost[2]
        ),
    )


def sds(shape, dtype):
    return jax.ShapeDtypeStruct(shape, dtype)


def fetch(pairs, sems):
    copies = [
        pltpu.make_async_copy(source, target, sems.at[index])
        for index, (source, target) in enumerate(pairs)
    ]
    for copy in copies:
        copy.start()
    return [copy.wait for copy in copies]


def chain_products(chain, device):
    product, products = None, []
    for level in range(LEVELS):
        bit = jnp.bitwise_and(jnp.right_shift(device, level), 1)
        half = chain[0, level, pl.ds(pl.multiple_of(bit * RANK, RANK), RANK), :]
        product = half if product is None else mm(product, half).astype(BF16)
        products.append(product)
    return products


def rise_kernel(
    points,
    inputs,
    order,
    cot,
    basis,
    transfer,
    chain,
    joined,
    coeffs,
    send,
    raw_v,
    order_v,
    cot_v,
    basis_v,
    transfer_v,
    chain_v,
    joined_v,
    coeffs_v,
    source_v,
    in_sems,
    joined_sems,
    coeff_sems,
):
    waits = fetch(
        (
            (points, raw_v.at[pl.ds(DIM, DIM)]),
            (inputs, raw_v.at[pl.ds(0, DIM)]),
            (order, order_v),
            (chain, chain_v),
            (cot, cot_v),
            (basis, basis_v),
            (transfer, transfer_v),
        ),
        in_sems,
    )
    device = lax.axis_index("pts")
    base = device * (LEAVES * ROWS)
    for wait in waits[:4]:
        wait()
    products = chain_products(chain_v, device)
    for index in range(4):
        low = raw_v[:, pl.ds(index * 512, ROWS)].T
        high = raw_v[:, pl.ds(index * 512 + ROWS, ROWS)].T
        source_v[index] = jnp.concatenate([low, high], axis=1)
    lane = lanes(ROWS, ROWS).astype(F32).astype(BF16)
    one, zero = jnp.ones((), BF16), jnp.zeros((), BF16)
    joined_copies = []
    for leaf in range(LEAVES):
        pieces = [order_v[pl.ds(2 * leaf + index, 1), :] - base for index in range(2)]
        row = jnp.concatenate(pieces, axis=1)
        low = jnp.bitwise_and(row, 255).astype(F32)
        high = jnp.right_shift(row, 8).astype(F32)
        low = jnp.broadcast_to(low, (128, ROWS)).T.astype(BF16)
        high = jnp.broadcast_to(high, (128, ROWS)).T
        hit = jnp.where(jnp.concatenate([low, low], axis=1) == lane, one, zero)
        value = jnp.zeros((ROWS, 128), F32)
        for index in range(4):
            found = mm(hit, source_v[index])
            value = jnp.where(high == 2.0 * index, found[:, :128], value)
            value = jnp.where(high == 2.0 * index + 1.0, found[:, 128:], value)
        joined_v[leaf] = value.astype(BF16)
        copy = pltpu.make_async_copy(joined_v.at[leaf], joined.at[leaf], joined_sems.at[leaf])
        copy.start()
        joined_copies.append(copy)
    for wait in waits[4:]:
        wait()
    now = []
    for leaf in range(LEAVES):
        theirs = cot_v[:, pl.ds(leaf * ROWS, ROWS)]
        pair = jnp.concatenate([joined_v[leaf].T[:DIM], theirs], axis=0)
        now.append(mm(pair, basis_v[leaf]))
    offset, done, level = 0, 0, 0
    coeff_copies = []
    while len(now) > 1:
        for node, value in enumerate(now):
            coeffs_v[done + node] = value
        span = pl.ds(done, len(now))
        copy = pltpu.make_async_copy(coeffs_v.at[span], coeffs.at[span], coeff_sems.at[level])
        copy.start()
        coeff_copies.append(copy)
        done += len(now)
        level += 1
        now = [
            mm2(jnp.concatenate([now[2 * n], now[2 * n + 1]], axis=1), transfer_v[offset + n])
            for n in range(len(now) // 2)
        ]
        offset += len(now)
    above = mm(now[0].astype(BF16), jnp.concatenate(products, axis=1))
    parts = [now[0]]
    parts += [above[:, level * RANK : (level + 1) * RANK] for level in range(LEVELS)]
    parts = [part.reshape(MEMBERS, SHARE, RANK) for part in parts]
    parts.append(jnp.zeros((MEMBERS, SLAB - 5 * SHARE, RANK), F32))
    send[...] = jnp.concatenate(parts, axis=1).astype(BF16)
    for copy in joined_copies + coeff_copies:
        copy.wait()


def couple_kernel(
    coeffs,
    joined,
    cot,
    leaf_skel,
    local_skel,
    chain_skel,
    chain,
    after,
    couplings,
    chain_k,
    both,
    coeffs_v,
    joined_v,
    cot_v,
    leaf_v,
    local_v,
    skel_v,
    chain_v,
    couplings_v,
    chain_k_v,
    both_v,
    sems,
    out_sems,
):
    waits = fetch(
        (
            (cot, cot_v),
            (joined, joined_v),
            (chain_skel, skel_v),
            (chain, chain_v),
            (leaf_skel, leaf_v),
            (local_skel, local_v),
            (coeffs, coeffs_v),
        ),
        sems,
    )
    device = lax.axis_index("pts")
    for wait in waits[:4]:
        wait()
    for leaf in range(LEAVES):
        theirs = cot_v[:, pl.ds(leaf * ROWS, ROWS)].T
        both_v[leaf] = jnp.concatenate([joined_v[leaf][:, :DIM], theirs], axis=1)
    done = fetch(((both_v, both),), out_sems)
    products = chain_products(chain_v, device)
    for level in range(LEVELS):
        bit = jnp.bitwise_and(jnp.right_shift(device, level), 1)
        value = kappa(skel_v[0, level, 1 - bit], skel_v[0, level, bit]).astype(BF16)
        if level > 0:
            value = mm(value, products[level - 1], NT).astype(BF16)
        chain_k_v[level] = value
    chain_k_v[LEVELS] = products[LEVELS - 1].T
    done += fetch(((chain_k_v, chain_k),), out_sems.at[pl.ds(1, 1)])
    for wait in waits[4:]:
        wait()
    for node in range(0, 14, 2):
        if node < 8:
            even, odd = leaf_v[node], leaf_v[node + 1]
        else:
            even, odd = local_v[node - 8], local_v[node - 7]
        near_k = kappa(even, odd).astype(BF16)
        for target, other, dims in ((node, node + 1, NT), (node + 1, node, NN)):
            couplings_v[target] = mm2(coeffs_v[other], near_k, dims)
    done += fetch(((couplings_v, couplings),), out_sems.at[pl.ds(2, 1)])
    for wait in done:
        wait()


def part(received, member, index):
    return received[member].astype(F32)[index * SHARE : (index + 1) * SHARE]


def level_sums(received, index):
    sums = [part(received, member, index) for member in range(MEMBERS)]
    for _ in range(index):
        sums = [sums[2 * n] + sums[2 * n + 1] for n in range(len(sums) // 2)]
    return sums


def total_kernel(received, send):
    total = level_sums(received, LEVELS)[0]
    total = jnp.concatenate([total, jnp.zeros_like(total)], axis=0).astype(BF16)
    for group in range(GROUPS):
        send[group] = total


def reply_kernel(received, totals, top_skel, reply):
    flat = jnp.concatenate([totals[group] for group in range(GROUPS)], axis=1)
    group = jnp.right_shift(lax.axis_index("pts"), LEVELS)
    (mine,) = extended(top_skel[group], False, True)
    top_k = []
    for other in range(GROUPS):
        (theirs,) = extended(top_skel[other], True, False)
        value = jnp.exp2(mm(theirs.T, mine) * EXPO)
        top_k.append(jnp.where(group == other, 0.0, value).astype(BF16))
    field = mm(flat, jnp.concatenate(top_k, axis=0))[:SHARE]
    levels = [level_sums(received, level) for level in range(LEVELS)]
    blank = jnp.zeros((SHARE, RANK), F32)
    for member in range(MEMBERS):
        rows = [levels[level][(member >> level) ^ 1] for level in range(LEVELS)]
        reply[member] = jnp.concatenate(rows + [field, blank], axis=0).astype(BF16)


def down_kernel(
    replies, chain_k, transfer, couplings, both, basis, near, give, output, keep
):
    core = lax.axis_index("rhs")
    table = replies[...].astype(F32)
    got = [
        table[:, index * SHARE : (index + 1) * SHARE].reshape(RANK, RANK)
        for index in range(LEVELS + 1)
    ]
    rows = jnp.concatenate([part.astype(BF16) for part in got], axis=1)
    field = mm(rows, chain_k[...].reshape((LEVELS + 1) * RANK, RANK))
    now = [field]
    for start, count, offset in ((6, 1, 12), (4, 2, 8), (0, 4, 0)):
        below = []
        for node in range(count):
            spread = mm2(now[node], transfer[start + node], NT)
            for child in range(2):
                rows = spread[:, child * RANK : (child + 1) * RANK]
                below.append(couplings[offset + 2 * node + child] + rows)
        now = below
    away = pl.multiple_of((1 - core) * RANK, RANK)
    stay = pl.multiple_of(core * RANK, RANK)
    for leaf in range(LEAVES):
        swapped = jnp.concatenate([now[leaf][DIM:], now[leaf][:DIM]], axis=0)
        terms = jnp.concatenate(split(swapped), axis=0)
        for target, first in ((give, away), (keep, stay)):
            rows = both[leaf, pl.ds(first, RANK), :]
            target[leaf] = mm(jnp.concatenate([rows, rows], axis=1), terms).astype(target.dtype)
    for leaf in range(LEAVES):
        far = mm(now[leaf][:DIM].astype(BF16), basis[leaf], NT)
        output[:, pl.ds(leaf * ROWS, ROWS)] = (near[leaf] + far).astype(BF16)


def near_kernel(
    ids,
    valid,
    swap_a,
    own,
    swap_b,
    after,
    near,
    ids_v,
    valid_v,
    swap_a_v,
    own_v,
    swap_b_v,
    left,
    right,
    values,
    near_v,
    sems,
    near_sems,
):
    waits = fetch(
        ((own, own_v), (swap_a, swap_a_v), (swap_b, swap_b_v), (ids, ids_v), (valid, valid_v)),
        sems,
    )
    lane = lanes(ROWS)
    device = lax.axis_index("pts")
    odd = jnp.bitwise_and(device, 1)
    places = ((2 - 2 * odd) * LEAVES, LEAVES, 2 * odd * LEAVES)
    for wait, index, block in ((0, 1, own_v), (1, 0, swap_a_v), (2, 2, swap_b_v)):
        waits[wait]()
        for leaf in range(LEAVES):
            value = block[leaf]
            turned = value.T
            made = norm_rows(turned[DIM:], index == 1, True)
            spare = jnp.concatenate([made[-1].T, jnp.zeros((ROWS, 112), F32)], axis=1)
            values[places[index] + leaf] = turned[:DIM]
            right[places[index] + leaf] = jnp.where(
                lane < DIM, spare, value.astype(F32)
            ).astype(BF16)
            if index == 1:
                blank = jnp.zeros((DIM - 16, ROWS), BF16)
                left[leaf] = jnp.concatenate(
                    [made[0].astype(BF16), blank, turned[DIM:]], axis=0
                )
    shift = (device - 1) * LEAVES
    waits[3]()
    waits[4]()

    def body(leaf, carry):
        mine = left[leaf]
        total = jnp.zeros((DIM, ROWS), F32)
        for start in range(0, SLOTS, 4):
            tiles, others = [], []
            for slot in range(start, start + 4):
                where = ids_v[leaf, slot] - shift
                used = jnp.full((1, ROWS), valid_v[leaf, slot], jnp.int32).astype(F32).astype(BF16)
                tiles.append(jnp.exp2(mm(right[where], mine) * EXPO).astype(BF16))
                others.append(values[where] * used)
            total = total + mm(jnp.concatenate(others, axis=1), jnp.concatenate(tiles, axis=0))
        near_v[leaf] = total
        pltpu.make_async_copy(near_v.at[leaf], near.at[leaf], near_sems.at[leaf]).start()
        return carry

    lax.fori_loop(0, LEAVES, body, 0)
    for leaf in range(LEAVES):
        pltpu.make_async_copy(near_v.at[leaf], near.at[leaf], near_sems.at[leaf]).wait()


def local(
    points,
    inputs,
    cotangent,
    order,
    near_ids,
    near_valid,
    leaf_basis,
    local_transfer,
    chain_transfer,
    leaf_skel,
    local_skel,
    chain_skel,
    top_skel,
):
    count = lax.axis_size("pts")
    block = (LEAVES, ROWS, 128)

    points, inputs, cot = points.T, inputs.T, cotangent.T
    leaf_skel, local_skel, chain_skel, top_skel = (
        jnp.swapaxes(skel, -1, -2) for skel in (leaf_skel, local_skel, chain_skel, top_skel)
    )
    order = order.reshape(2 * LEAVES, 128)
    joined, coeffs, send = call(
        rise_kernel,
        (
            sds(block, BF16),
            sds((14, RANK, RANK), F32),
            sds((MEMBERS, SLAB, RANK), BF16),
        ),
        [HBM] * 7,
        [
            pltpu.VMEM((2 * DIM, LEAVES * ROWS), BF16),
            pltpu.VMEM((2 * LEAVES, 128), jnp.int32),
            pltpu.VMEM((DIM, LEAVES * ROWS), BF16),
            pltpu.VMEM(block, BF16),
            pltpu.VMEM(local_transfer.shape, BF16),
            pltpu.VMEM(chain_transfer.shape, BF16),
            pltpu.VMEM(block, BF16),
            pltpu.VMEM((14, RANK, RANK), F32),
            pltpu.VMEM((4, ROWS, 256), BF16),
            pltpu.SemaphoreType.DMA((7,)),
            pltpu.SemaphoreType.DMA((LEAVES,)),
            pltpu.SemaphoreType.DMA((3,)),
        ],
        places=(HBM, HBM, VMEM),
    )(points, inputs, order, cot, leaf_basis, local_transfer, chain_transfer)

    groups = [[g * MEMBERS + i for i in range(MEMBERS)] for g in range(GROUPS)]
    across = [[g * MEMBERS + i for g in range(GROUPS)] for i in range(MEMBERS)]
    received = lax.all_to_all(send, "pts", 0, 0, axis_index_groups=groups, tiled=True)

    swaps = []
    for first in (0, 1):
        pairs = [(i, i + 1) for i in range(first, count - 1, 2)]
        swaps.append(lax.ppermute(joined, "pts", pairs + [(b, a) for a, b in pairs]))

    total = call(
        total_kernel, sds((GROUPS, 2 * SHARE, RANK), BF16), [VMEM], room=8
    )(received)
    totals = lax.all_to_all(total, "pts", 0, 0, axis_index_groups=across, tiled=True)

    tree = (14, RANK, RANK)
    square = (LEAVES, RANK, RANK)
    links = (LEVELS + 1, RANK, RANK)
    couplings, chain_k, both = call(
        couple_kernel,
        (sds(tree, F32), sds(links, BF16), sds(block, BF16)),
        [HBM] * 7 + [ANY],
        [
            pltpu.VMEM(tree, F32),
            pltpu.VMEM(block, BF16),
            pltpu.VMEM((DIM, LEAVES * ROWS), BF16),
            pltpu.VMEM(leaf_skel.shape, BF16),
            pltpu.VMEM(local_skel.shape, BF16),
            pltpu.VMEM(chain_skel.shape, BF16),
            pltpu.VMEM(chain_transfer.shape, BF16),
            pltpu.VMEM(tree, F32),
            pltpu.VMEM(links, BF16),
            pltpu.VMEM(block, BF16),
            pltpu.SemaphoreType.DMA((7,)),
            pltpu.SemaphoreType.DMA((3,)),
        ],
        cost=(2 * 10**9, 4 * 10**6, 10**6),
        places=(HBM,) * 3,
    )(coeffs, joined, cot, leaf_skel, local_skel, chain_skel, chain_transfer, total)

    reply = call(
        reply_kernel, sds((MEMBERS, SLAB, RANK), BF16), [VMEM] * 3, room=8
    )(received, totals, top_skel)
    replies = lax.all_to_all(reply, "pts", 0, 0, axis_index_groups=groups, tiled=True)

    near = call(
        near_kernel,
        sds((LEAVES, DIM, ROWS), F32),
        [HBM] * 5 + [ANY],
        [
            pltpu.SMEM((LEAVES, SLOTS), jnp.int32),
            pltpu.SMEM((LEAVES, SLOTS), jnp.int32),
            pltpu.VMEM(block, BF16),
            pltpu.VMEM(block, BF16),
            pltpu.VMEM(block, BF16),
            pltpu.VMEM((LEAVES, 128, ROWS), BF16),
            pltpu.VMEM((3 * LEAVES, ROWS, 128), BF16),
            pltpu.VMEM((3 * LEAVES, DIM, ROWS), BF16),
            pltpu.VMEM((LEAVES, DIM, ROWS), F32),
            pltpu.SemaphoreType.DMA((5,)),
            pltpu.SemaphoreType.DMA((LEAVES,)),
        ],
        cost=(5 * 10**10, 4 * 10**6, LEAVES * 800000),
        places=HBM,
        room=60,
    )(near_ids, near_valid, swaps[0], joined, swaps[1], reply)

    give, output, keep = call(
        down_kernel,
        (sds(square, BF16), sds((DIM, LEAVES * ROWS), BF16), sds(square, F32)),
        [VMEM] * 7,
        room=14,
    )(
        replies,
        chain_k,
        local_transfer,
        couplings,
        both,
        leaf_basis,
        near,
    )
    got = lax.ppermute(give, "rhs", [(0, 1), (1, 0)])
    basis_grad = (keep + got.astype(F32)).astype(BF16)
    return output.T, basis_grad


def solution(mesh):
    placed = (
        P("pts", None),
        P("pts", "rhs"),
        P("pts", "rhs"),
        P("pts"),
        P("pts", None),
        P("pts", None),
        P("pts", None, None),
        P("pts", None, None),
        P("pts", None, None, None),
        P("pts", None, None),
        P("pts", None, None),
        P("pts", None, None, None, None),
        P(),
    )
    return jax.shard_map(
        local,
        mesh=mesh,
        in_specs=placed,
        out_specs=(P("pts", "rhs"), P("pts", "rhs", None)),
        check_vma=False,
    )
```

```python
import math

import jax
import jax.numpy as jnp
from jax import lax
from jax.experimental import pallas as pl
from jax.experimental.pallas import tpu as pltpu
from jax.sharding import PartitionSpec as P

F32 = jnp.float32
BF16 = jnp.bfloat16

LEVELS = 4
MEMBERS = 16
GROUPS = 16
SLAB = 48
SHARE = 8
LEAVES = 8
ROWS = 256
RANK = 128
DIM = 64
SLOTS = 12

VMEM = pl.BlockSpec(memory_space=pltpu.VMEM)
ANY = pl.BlockSpec(memory_space=pl.ANY)
HBM = pl.BlockSpec(memory_space=pltpu.HBM)
NN = (((1,), (0,)), ((), ()))
NT = (((1,), (1,)), ((), ()))


def mm(a, b, dims=NN):
    return lax.dot_general(a, b, dims, preferred_element_type=F32)


def split(a):
    high = a.astype(BF16)
    return high, (a - high.astype(F32)).astype(BF16)


def mm2(a, b, dims=NN):
    high, low = split(a)
    along = dims[0][1][0]
    return mm(jnp.concatenate([high, low], axis=1), jnp.concatenate([b, b], axis=along), dims)


def lanes(rows, width=128):
    return lax.broadcasted_iota(jnp.int32, (rows, width), 1)


def norm_rows(pts, left, right):
    wide = pts.astype(F32)
    half = -0.5 * jnp.sum(wide * wide, axis=0, keepdims=True)
    first = half.astype(BF16).astype(F32)
    rest = half - first
    second = rest.astype(BF16).astype(F32)
    third = rest - second
    row = lax.broadcasted_iota(jnp.int32, (16, pts.shape[1]), 0)
    out = []
    for want, low, ones in ((left, 0, 3), (right, 3, 0)):
        if not want:
            continue
        value = jnp.where((row >= ones) & (row < ones + 3), 1.0, 0.0)
        for offset, term in enumerate((first, second, third)):
            value = jnp.where(row == low + offset, term, value)
        out.append(value)
    return out


def extended(pts, left, right):
    blank = jnp.zeros((128 - DIM - 16, pts.shape[1]), BF16)
    return [
        jnp.concatenate([pts, rows.astype(BF16), blank], axis=0)
        for rows in norm_rows(pts, left, right)
    ]


EXPO = 4.0 / (DIM * math.log(2.0))


def kappa(left_pts, right_pts):
    (left,) = extended(left_pts, True, False)
    (right,) = extended(right_pts, False, True)
    return jnp.exp2(mm(left.T, right) * EXPO)


def call(kernel, outs, specs, scratch=(), cost=(0, 0, 0), places=None, room=60):
    return pl.pallas_call(
        kernel,
        out_shape=outs,
        in_specs=specs,
        out_specs=places or jax.tree.map(lambda _: VMEM, outs),
        scratch_shapes=list(scratch),
        compiler_params=pltpu.CompilerParams(vmem_limit_bytes=int(room * 2**20)),
        cost_estimate=pl.CostEstimate(
            flops=cost[0], bytes_accessed=cost[1], transcendentals=cost[2]
        ),
    )


def sds(shape, dtype):
    return jax.ShapeDtypeStruct(shape, dtype)


def fetch(pairs, sems):
    copies = [
        pltpu.make_async_copy(source, target, sems.at[index])
        for index, (source, target) in enumerate(pairs)
    ]
    for copy in copies:
        copy.start()
    return [copy.wait for copy in copies]


def chain_products(chain, device):
    product, products = None, []
    for level in range(LEVELS):
        bit = jnp.bitwise_and(jnp.right_shift(device, level), 1)
        half = chain[0, level, pl.ds(pl.multiple_of(bit * RANK, RANK), RANK), :]
        product = half if product is None else mm(product, half).astype(BF16)
        products.append(product)
    return products


def rise_kernel(
    points,
    inputs,
    order,
    cot,
    basis,
    transfer,
    chain,
    joined,
    coeffs,
    send,
    raw_v,
    order_v,
    cot_v,
    basis_v,
    transfer_v,
    chain_v,
    joined_v,
    coeffs_v,
    source_v,
    in_sems,
    joined_sems,
    coeff_sems,
):
    waits = fetch(
        (
            (points, raw_v.at[pl.ds(DIM, DIM)]),
            (inputs, raw_v.at[pl.ds(0, DIM)]),
            (order, order_v),
            (chain, chain_v),
            (cot, cot_v),
            (basis, basis_v),
            (transfer, transfer_v),
        ),
        in_sems,
    )
    device = lax.axis_index("pts")
    base = device * (LEAVES * ROWS)
    for wait in waits[:4]:
        wait()
    products = chain_products(chain_v, device)
    for index in range(4):
        low = raw_v[:, pl.ds(index * 512, ROWS)].T
        high = raw_v[:, pl.ds(index * 512 + ROWS, ROWS)].T
        source_v[index] = jnp.concatenate([low, high], axis=1)
    lane = lanes(ROWS, ROWS).astype(F32).astype(BF16)
    one, zero = jnp.ones((), BF16), jnp.zeros((), BF16)
    joined_copies = []
    for leaf in range(LEAVES):
        pieces = [order_v[pl.ds(2 * leaf + index, 1), :] - base for index in range(2)]
        row = jnp.concatenate(pieces, axis=1)
        low = jnp.bitwise_and(row, 255).astype(F32)
        high = jnp.right_shift(row, 8).astype(F32)
        low = jnp.broadcast_to(low, (128, ROWS)).T.astype(BF16)
        high = jnp.broadcast_to(high, (128, ROWS)).T
        hit = jnp.where(jnp.concatenate([low, low], axis=1) == lane, one, zero)
        value = jnp.zeros((ROWS, 128), F32)
        for index in range(4):
            found = mm(hit, source_v[index])
            value = jnp.where(high == 2.0 * index, found[:, :128], value)
            value = jnp.where(high == 2.0 * index + 1.0, found[:, 128:], value)
        joined_v[leaf] = value.astype(BF16)
        copy = pltpu.make_async_copy(joined_v.at[leaf], joined.at[leaf], joined_sems.at[leaf])
        copy.start()
        joined_copies.append(copy)
    for wait in waits[4:]:
        wait()
    now = []
    for leaf in range(LEAVES):
        theirs = cot_v[:, pl.ds(leaf * ROWS, ROWS)]
        pair = jnp.concatenate([joined_v[leaf].T[:DIM], theirs], axis=0)
        now.append(mm(pair, basis_v[leaf]))
    offset, done, level = 0, 0, 0
    coeff_copies = []
    while len(now) > 1:
        for node, value in enumerate(now):
            coeffs_v[done + node] = value
        span = pl.ds(done, len(now))
        copy = pltpu.make_async_copy(coeffs_v.at[span], coeffs.at[span], coeff_sems.at[level])
        copy.start()
        coeff_copies.append(copy)
        done += len(now)
        level += 1
        now = [
            mm2(jnp.concatenate([now[2 * n], now[2 * n + 1]], axis=1), transfer_v[offset + n])
            for n in range(len(now) // 2)
        ]
        offset += len(now)
    above = mm(now[0].astype(BF16), jnp.concatenate(products, axis=1))
    parts = [now[0]]
    parts += [above[:, level * RANK : (level + 1) * RANK] for level in range(LEVELS)]
    parts = [part.reshape(MEMBERS, SHARE, RANK) for part in parts]
    parts.append(jnp.zeros((MEMBERS, SLAB - 5 * SHARE, RANK), F32))
    send[...] = jnp.concatenate(parts, axis=1).astype(BF16)
    for copy in joined_copies + coeff_copies:
        copy.wait()


def couple_kernel(
    coeffs,
    joined,
    cot,
    leaf_skel,
    local_skel,
    chain_skel,
    chain,
    after,
    couplings,
    chain_k,
    both,
    coeffs_v,
    joined_v,
    cot_v,
    leaf_v,
    local_v,
    skel_v,
    chain_v,
    couplings_v,
    chain_k_v,
    both_v,
    sems,
    out_sems,
):
    waits = fetch(
        (
            (cot, cot_v),
            (joined, joined_v),
            (chain_skel, skel_v),
            (chain, chain_v),
            (leaf_skel, leaf_v),
            (local_skel, local_v),
            (coeffs, coeffs_v),
        ),
        sems,
    )
    device = lax.axis_index("pts")
    for wait in waits[:4]:
        wait()
    for leaf in range(LEAVES):
        theirs = cot_v[:, pl.ds(leaf * ROWS, ROWS)].T
        both_v[leaf] = jnp.concatenate([joined_v[leaf][:, :DIM], theirs], axis=1)
    done = fetch(((both_v, both),), out_sems)
    products = chain_products(chain_v, device)
    for level in range(LEVELS):
        bit = jnp.bitwise_and(jnp.right_shift(device, level), 1)
        value = kappa(skel_v[0, level, 1 - bit], skel_v[0, level, bit]).astype(BF16)
        if level > 0:
            value = mm(value, products[level - 1], NT).astype(BF16)
        chain_k_v[level] = value
    chain_k_v[LEVELS] = products[LEVELS - 1].T
    done += fetch(((chain_k_v, chain_k),), out_sems.at[pl.ds(1, 1)])
    for wait in waits[4:]:
        wait()
    for node in range(0, 14, 2):
        if node < 8:
            even, odd = leaf_v[node], leaf_v[node + 1]
        else:
            even, odd = local_v[node - 8], local_v[node - 7]
        near_k = kappa(even, odd).astype(BF16)
        for target, other, dims in ((node, node + 1, NT), (node + 1, node, NN)):
            couplings_v[target] = mm2(coeffs_v[other], near_k, dims)
    done += fetch(((couplings_v, couplings),), out_sems.at[pl.ds(2, 1)])
    for wait in done:
        wait()


def part(received, member, index):
    return received[member].astype(F32)[index * SHARE : (index + 1) * SHARE]


def level_sums(received, index):
    sums = [part(received, member, index) for member in range(MEMBERS)]
    for _ in range(index):
        sums = [sums[2 * n] + sums[2 * n + 1] for n in range(len(sums) // 2)]
    return sums


def total_kernel(received, send):
    total = level_sums(received, LEVELS)[0]
    total = jnp.concatenate([total, jnp.zeros_like(total)], axis=0).astype(BF16)
    for group in range(GROUPS):
        send[group] = total


def reply_kernel(received, totals, top_skel, reply):
    flat = jnp.concatenate([totals[group] for group in range(GROUPS)], axis=1)
    group = jnp.right_shift(lax.axis_index("pts"), LEVELS)
    (mine,) = extended(top_skel[group], False, True)
    top_k = []
    for other in range(GROUPS):
        (theirs,) = extended(top_skel[other], True, False)
        value = jnp.exp2(mm(theirs.T, mine) * EXPO)
        top_k.append(jnp.where(group == other, 0.0, value).astype(BF16))
    field = mm(flat, jnp.concatenate(top_k, axis=0))[:SHARE]
    levels = [level_sums(received, level) for level in range(LEVELS)]
    blank = jnp.zeros((SHARE, RANK), F32)
    for member in range(MEMBERS):
        rows = [levels[level][(member >> level) ^ 1] for level in range(LEVELS)]
        reply[member] = jnp.concatenate(rows + [field, blank], axis=0).astype(BF16)


def down_kernel(
    replies, chain_k, transfer, couplings, both, fields, give, keep
):
    core = lax.axis_index("rhs")
    table = replies[...].astype(F32)
    got = [
        table[:, index * SHARE : (index + 1) * SHARE].reshape(RANK, RANK)
        for index in range(LEVELS + 1)
    ]
    rows = jnp.concatenate([part.astype(BF16) for part in got], axis=1)
    field = mm(rows, chain_k[...].reshape((LEVELS + 1) * RANK, RANK))
    now = [field]
    for start, count, offset in ((6, 1, 12), (4, 2, 8), (0, 4, 0)):
        below = []
        for node in range(count):
            spread = mm2(now[node], transfer[start + node], NT)
            for child in range(2):
                rows = spread[:, child * RANK : (child + 1) * RANK]
                below.append(couplings[offset + 2 * node + child] + rows)
        now = below
    away = pl.multiple_of((1 - core) * RANK, RANK)
    stay = pl.multiple_of(core * RANK, RANK)
    for leaf in range(LEAVES):
        swapped = jnp.concatenate([now[leaf][DIM:], now[leaf][:DIM]], axis=0)
        terms = jnp.concatenate(split(swapped), axis=0)
        for target, first in ((give, away), (keep, stay)):
            rows = both[leaf, pl.ds(first, RANK), :]
            target[leaf] = mm(jnp.concatenate([rows, rows], axis=1), terms).astype(target.dtype)
    for leaf in range(LEAVES):
        fields[leaf] = now[leaf][:DIM].astype(BF16)


def finish_kernel(fields, basis, near, output):
    for leaf in range(LEAVES):
        far = mm(fields[leaf], basis[leaf], NT)
        output[:, pl.ds(leaf * ROWS, ROWS)] = (near[leaf] + far).astype(BF16)


def near_kernel(
    ids,
    valid,
    swap_a,
    own,
    swap_b,
    after,
    near,
    ids_v,
    valid_v,
    swap_a_v,
    own_v,
    swap_b_v,
    left,
    right,
    values,
    near_v,
    sems,
    near_sems,
):
    waits = fetch(
        ((own, own_v), (swap_a, swap_a_v), (swap_b, swap_b_v), (ids, ids_v), (valid, valid_v)),
        sems,
    )
    lane = lanes(ROWS)
    device = lax.axis_index("pts")
    odd = jnp.bitwise_and(device, 1)
    places = ((2 - 2 * odd) * LEAVES, LEAVES, 2 * odd * LEAVES)
    for wait, index, block in ((0, 1, own_v), (1, 0, swap_a_v), (2, 2, swap_b_v)):
        waits[wait]()
        for leaf in range(LEAVES):
            value = block[leaf]
            turned = value.T
            made = norm_rows(turned[DIM:], index == 1, True)
            spare = jnp.concatenate([made[-1].T, jnp.zeros((ROWS, 112), F32)], axis=1)
            values[places[index] + leaf] = turned[:DIM]
            right[places[index] + leaf] = jnp.where(
                lane < DIM, spare, value.astype(F32)
            ).astype(BF16)
            if index == 1:
                blank = jnp.zeros((DIM - 16, ROWS), BF16)
                left[leaf] = jnp.concatenate(
                    [made[0].astype(BF16), blank, turned[DIM:]], axis=0
                )
    shift = (device - 1) * LEAVES
    waits[3]()
    waits[4]()

    def body(leaf, carry):
        mine = left[leaf]
        total = jnp.zeros((DIM, ROWS), F32)
        for start in range(0, SLOTS, 4):
            tiles, others = [], []
            for slot in range(start, start + 4):
                where = ids_v[leaf, slot] - shift
                used = jnp.full((1, ROWS), valid_v[leaf, slot], jnp.int32).astype(F32).astype(BF16)
                tiles.append(jnp.exp2(mm(right[where], mine) * EXPO).astype(BF16))
                others.append(values[where] * used)
            total = total + mm(jnp.concatenate(others, axis=1), jnp.concatenate(tiles, axis=0))
        near_v[leaf] = total
        pltpu.make_async_copy(near_v.at[leaf], near.at[leaf], near_sems.at[leaf]).start()
        return carry

    lax.fori_loop(0, LEAVES, body, 0)
    for leaf in range(LEAVES):
        pltpu.make_async_copy(near_v.at[leaf], near.at[leaf], near_sems.at[leaf]).wait()


def local(
    points,
    inputs,
    cotangent,
    order,
    near_ids,
    near_valid,
    leaf_basis,
    local_transfer,
    chain_transfer,
    leaf_skel,
    local_skel,
    chain_skel,
    top_skel,
):
    count = lax.axis_size("pts")
    block = (LEAVES, ROWS, 128)

    points, inputs, cot = points.T, inputs.T, cotangent.T
    leaf_skel, local_skel, chain_skel, top_skel = (
        jnp.swapaxes(skel, -1, -2) for skel in (leaf_skel, local_skel, chain_skel, top_skel)
    )
    order = order.reshape(2 * LEAVES, 128)
    joined, coeffs, send = call(
        rise_kernel,
        (
            sds(block, BF16),
            sds((14, RANK, RANK), F32),
            sds((MEMBERS, SLAB, RANK), BF16),
        ),
        [HBM] * 7,
        [
            pltpu.VMEM((2 * DIM, LEAVES * ROWS), BF16),
            pltpu.VMEM((2 * LEAVES, 128), jnp.int32),
            pltpu.VMEM((DIM, LEAVES * ROWS), BF16),
            pltpu.VMEM(block, BF16),
            pltpu.VMEM(local_transfer.shape, BF16),
            pltpu.VMEM(chain_transfer.shape, BF16),
            pltpu.VMEM(block, BF16),
            pltpu.VMEM((14, RANK, RANK), F32),
            pltpu.VMEM((4, ROWS, 256), BF16),
            pltpu.SemaphoreType.DMA((7,)),
            pltpu.SemaphoreType.DMA((LEAVES,)),
            pltpu.SemaphoreType.DMA((3,)),
        ],
        places=(HBM, HBM, VMEM),
    )(points, inputs, order, cot, leaf_basis, local_transfer, chain_transfer)

    groups = [[g * MEMBERS + i for i in range(MEMBERS)] for g in range(GROUPS)]
    across = [[g * MEMBERS + i for g in range(GROUPS)] for i in range(MEMBERS)]
    received = lax.all_to_all(send, "pts", 0, 0, axis_index_groups=groups, tiled=True)

    swaps = []
    for first in (0, 1):
        pairs = [(i, i + 1) for i in range(first, count - 1, 2)]
        swaps.append(lax.ppermute(joined, "pts", pairs + [(b, a) for a, b in pairs]))

    total = call(
        total_kernel, sds((GROUPS, 2 * SHARE, RANK), BF16), [VMEM], room=8
    )(received)
    totals = lax.all_to_all(total, "pts", 0, 0, axis_index_groups=across, tiled=True)

    tree = (14, RANK, RANK)
    square = (LEAVES, RANK, RANK)
    links = (LEVELS + 1, RANK, RANK)
    couplings, chain_k, both = call(
        couple_kernel,
        (sds(tree, F32), sds(links, BF16), sds(block, BF16)),
        [HBM] * 7 + [ANY],
        [
            pltpu.VMEM(tree, F32),
            pltpu.VMEM(block, BF16),
            pltpu.VMEM((DIM, LEAVES * ROWS), BF16),
            pltpu.VMEM(leaf_skel.shape, BF16),
            pltpu.VMEM(local_skel.shape, BF16),
            pltpu.VMEM(chain_skel.shape, BF16),
            pltpu.VMEM(chain_transfer.shape, BF16),
            pltpu.VMEM(tree, F32),
            pltpu.VMEM(links, BF16),
            pltpu.VMEM(block, BF16),
            pltpu.SemaphoreType.DMA((7,)),
            pltpu.SemaphoreType.DMA((3,)),
        ],
        cost=(2 * 10**9, 4 * 10**6, 10**6),
        places=(HBM,) * 3,
    )(coeffs, joined, cot, leaf_skel, local_skel, chain_skel, chain_transfer, total)

    reply = call(
        reply_kernel, sds((MEMBERS, SLAB, RANK), BF16), [VMEM] * 3, room=8
    )(received, totals, top_skel)
    replies = lax.all_to_all(reply, "pts", 0, 0, axis_index_groups=groups, tiled=True)

    near = call(
        near_kernel,
        sds((LEAVES, DIM, ROWS), F32),
        [HBM] * 5 + [ANY],
        [
            pltpu.SMEM((LEAVES, SLOTS), jnp.int32),
            pltpu.SMEM((LEAVES, SLOTS), jnp.int32),
            pltpu.VMEM(block, BF16),
            pltpu.VMEM(block, BF16),
            pltpu.VMEM(block, BF16),
            pltpu.VMEM((LEAVES, 128, ROWS), BF16),
            pltpu.VMEM((3 * LEAVES, ROWS, 128), BF16),
            pltpu.VMEM((3 * LEAVES, DIM, ROWS), BF16),
            pltpu.VMEM((LEAVES, DIM, ROWS), F32),
            pltpu.SemaphoreType.DMA((5,)),
            pltpu.SemaphoreType.DMA((LEAVES,)),
        ],
        cost=(5 * 10**10, 4 * 10**6, LEAVES * 800000),
        places=HBM,
        room=14,
    )(near_ids, near_valid, swaps[0], joined, swaps[1], reply)

    fields, give, keep = call(
        down_kernel,
        (sds((LEAVES, DIM, RANK), BF16), sds(square, BF16), sds(square, F32)),
        [VMEM] * 5,
        room=14,
    )(replies, chain_k, local_transfer, couplings, both)
    got = lax.ppermute(give, "rhs", [(0, 1), (1, 0)])
    output = call(
        finish_kernel,
        sds((DIM, LEAVES * ROWS), BF16),
        [VMEM] * 3,
        cost=(3 * 10**9, 2 * 10**6, 0),
        room=14,
    )(fields, leaf_basis, near)
    basis_grad = (keep + got.astype(F32)).astype(BF16)
    return output.T, basis_grad


def solution(mesh):
    placed = (
        P("pts", None),
        P("pts", "rhs"),
        P("pts", "rhs"),
        P("pts"),
        P("pts", None),
        P("pts", None),
        P("pts", None, None),
        P("pts", None, None),
        P("pts", None, None, None),
        P("pts", None, None),
        P("pts", None, None),
        P("pts", None, None, None, None),
        P(),
    )
    return jax.shard_map(
        local,
        mesh=mesh,
        in_specs=placed,
        out_specs=(P("pts", "rhs"), P("pts", "rhs", None)),
        check_vma=False,
    )
```

```python
import math

import jax
import jax.numpy as jnp
from jax import lax
from jax.experimental import pallas as pl
from jax.experimental.pallas import tpu as pltpu
from jax.sharding import PartitionSpec as P

F32 = jnp.float32
BF16 = jnp.bfloat16

LEVELS = 4
MEMBERS = 16
GROUPS = 16
SLAB = 48
SHARE = 8
LEAVES = 8
ROWS = 256
RANK = 128
DIM = 64
SLOTS = 12

VMEM = pl.BlockSpec(memory_space=pltpu.VMEM)
ANY = pl.BlockSpec(memory_space=pl.ANY)
HBM = pl.BlockSpec(memory_space=pltpu.HBM)
NN = (((1,), (0,)), ((), ()))
NT = (((1,), (1,)), ((), ()))


def mm(a, b, dims=NN):
    return lax.dot_general(a, b, dims, preferred_element_type=F32)


def split(a):
    high = a.astype(BF16)
    return high, (a - high.astype(F32)).astype(BF16)


def mm2(a, b, dims=NN):
    high, low = split(a)
    along = dims[0][1][0]
    return mm(jnp.concatenate([high, low], axis=1), jnp.concatenate([b, b], axis=along), dims)


def lanes(rows, width=128):
    return lax.broadcasted_iota(jnp.int32, (rows, width), 1)


def norm_rows(pts, left, right):
    wide = pts.astype(F32)
    half = -0.5 * jnp.sum(wide * wide, axis=0, keepdims=True)
    first = half.astype(BF16).astype(F32)
    rest = half - first
    second = rest.astype(BF16).astype(F32)
    third = rest - second
    row = lax.broadcasted_iota(jnp.int32, (16, pts.shape[1]), 0)
    out = []
    for want, low, ones in ((left, 0, 3), (right, 3, 0)):
        if not want:
            continue
        value = jnp.where((row >= ones) & (row < ones + 3), 1.0, 0.0)
        for offset, term in enumerate((first, second, third)):
            value = jnp.where(row == low + offset, term, value)
        out.append(value)
    return out


def extended(pts, left, right):
    blank = jnp.zeros((128 - DIM - 16, pts.shape[1]), BF16)
    return [
        jnp.concatenate([pts, rows.astype(BF16), blank], axis=0)
        for rows in norm_rows(pts, left, right)
    ]


EXPO = 4.0 / (DIM * math.log(2.0))


def kappa(left_pts, right_pts):
    (left,) = extended(left_pts, True, False)
    (right,) = extended(right_pts, False, True)
    return jnp.exp2(mm(left.T, right) * EXPO)


def call(kernel, outs, specs, scratch=(), cost=(0, 0, 0), places=None, room=60):
    return pl.pallas_call(
        kernel,
        out_shape=outs,
        in_specs=specs,
        out_specs=places or jax.tree.map(lambda _: VMEM, outs),
        scratch_shapes=list(scratch),
        compiler_params=pltpu.CompilerParams(vmem_limit_bytes=int(room * 2**20)),
        cost_estimate=pl.CostEstimate(
            flops=cost[0], bytes_accessed=cost[1], transcendentals=cost[2]
        ),
    )


def sds(shape, dtype):
    return jax.ShapeDtypeStruct(shape, dtype)


def fetch(pairs, sems):
    copies = [
        pltpu.make_async_copy(source, target, sems.at[index])
        for index, (source, target) in enumerate(pairs)
    ]
    for copy in copies:
        copy.start()
    return [copy.wait for copy in copies]


def chain_products(chain, device):
    product, products = None, []
    for level in range(LEVELS):
        bit = jnp.bitwise_and(jnp.right_shift(device, level), 1)
        half = chain[0, level, pl.ds(pl.multiple_of(bit * RANK, RANK), RANK), :]
        product = half if product is None else mm(product, half).astype(BF16)
        products.append(product)
    return products


def rise_kernel(
    points,
    inputs,
    order,
    cot,
    basis,
    transfer,
    chain,
    joined,
    coeffs,
    send,
    raw_v,
    order_v,
    cot_v,
    basis_v,
    transfer_v,
    chain_v,
    joined_v,
    coeffs_v,
    source_v,
    in_sems,
    joined_sems,
    coeff_sems,
):
    waits = fetch(
        (
            (points, raw_v.at[pl.ds(DIM, DIM)]),
            (inputs, raw_v.at[pl.ds(0, DIM)]),
            (order, order_v),
            (chain, chain_v),
            (cot, cot_v),
            (basis, basis_v),
            (transfer, transfer_v),
        ),
        in_sems,
    )
    device = lax.axis_index("pts")
    base = device * (LEAVES * ROWS)
    for wait in waits[:4]:
        wait()
    products = chain_products(chain_v, device)
    for index in range(4):
        low = raw_v[:, pl.ds(index * 512, ROWS)].T
        high = raw_v[:, pl.ds(index * 512 + ROWS, ROWS)].T
        source_v[index] = jnp.concatenate([low, high], axis=1)
    lane = lanes(ROWS, ROWS).astype(F32).astype(BF16)
    one, zero = jnp.ones((), BF16), jnp.zeros((), BF16)
    joined_copies = []
    for leaf in range(LEAVES):
        pieces = [order_v[pl.ds(2 * leaf + index, 1), :] - base for index in range(2)]
        row = jnp.concatenate(pieces, axis=1)
        low = jnp.bitwise_and(row, 255).astype(F32)
        high = jnp.right_shift(row, 8).astype(F32)
        low = jnp.broadcast_to(low, (128, ROWS)).T.astype(BF16)
        high = jnp.broadcast_to(high, (128, ROWS)).T
        hit = jnp.where(jnp.concatenate([low, low], axis=1) == lane, one, zero)
        value = jnp.zeros((ROWS, 128), F32)
        for index in range(4):
            found = mm(hit, source_v[index])
            value = jnp.where(high == 2.0 * index, found[:, :128], value)
            value = jnp.where(high == 2.0 * index + 1.0, found[:, 128:], value)
        joined_v[leaf] = value.astype(BF16)
        copy = pltpu.make_async_copy(joined_v.at[leaf], joined.at[leaf], joined_sems.at[leaf])
        copy.start()
        joined_copies.append(copy)
    for wait in waits[4:]:
        wait()
    now = []
    for leaf in range(LEAVES):
        theirs = cot_v[:, pl.ds(leaf * ROWS, ROWS)]
        pair = jnp.concatenate([joined_v[leaf].T[:DIM], theirs], axis=0)
        now.append(mm(pair, basis_v[leaf]))
    offset, done, level = 0, 0, 0
    coeff_copies = []
    while len(now) > 1:
        for node, value in enumerate(now):
            coeffs_v[done + node] = value
        span = pl.ds(done, len(now))
        copy = pltpu.make_async_copy(coeffs_v.at[span], coeffs.at[span], coeff_sems.at[level])
        copy.start()
        coeff_copies.append(copy)
        done += len(now)
        level += 1
        now = [
            mm2(jnp.concatenate([now[2 * n], now[2 * n + 1]], axis=1), transfer_v[offset + n])
            for n in range(len(now) // 2)
        ]
        offset += len(now)
    above = mm(now[0].astype(BF16), jnp.concatenate(products, axis=1))
    parts = [now[0]]
    parts += [above[:, level * RANK : (level + 1) * RANK] for level in range(LEVELS)]
    parts = [part.reshape(MEMBERS, SHARE, RANK) for part in parts]
    parts.append(jnp.zeros((MEMBERS, SLAB - 5 * SHARE, RANK), F32))
    send[...] = jnp.concatenate(parts, axis=1).astype(BF16)
    for copy in joined_copies + coeff_copies:
        copy.wait()


def couple_kernel(
    coeffs,
    joined,
    cot,
    leaf_skel,
    local_skel,
    chain_skel,
    chain,
    after,
    couplings,
    chain_k,
    both,
    coeffs_v,
    joined_v,
    cot_v,
    leaf_v,
    local_v,
    skel_v,
    chain_v,
    couplings_v,
    chain_k_v,
    both_v,
    sems,
    out_sems,
):
    waits = fetch(
        (
            (cot, cot_v),
            (joined, joined_v),
            (chain_skel, skel_v),
            (chain, chain_v),
            (leaf_skel, leaf_v),
            (local_skel, local_v),
            (coeffs, coeffs_v),
        ),
        sems,
    )
    device = lax.axis_index("pts")
    for wait in waits[:4]:
        wait()
    for leaf in range(LEAVES):
        theirs = cot_v[:, pl.ds(leaf * ROWS, ROWS)].T
        both_v[leaf] = jnp.concatenate([joined_v[leaf][:, :DIM], theirs], axis=1)
    done = fetch(((both_v, both),), out_sems)
    products = chain_products(chain_v, device)
    for level in range(LEVELS):
        bit = jnp.bitwise_and(jnp.right_shift(device, level), 1)
        value = kappa(skel_v[0, level, 1 - bit], skel_v[0, level, bit]).astype(BF16)
        if level > 0:
            value = mm(value, products[level - 1], NT).astype(BF16)
        chain_k_v[level] = value
    chain_k_v[LEVELS] = products[LEVELS - 1].T
    done += fetch(((chain_k_v, chain_k),), out_sems.at[pl.ds(1, 1)])
    for wait in waits[4:]:
        wait()
    for node in range(0, 14, 2):
        if node < 8:
            even, odd = leaf_v[node], leaf_v[node + 1]
        else:
            even, odd = local_v[node - 8], local_v[node - 7]
        near_k = kappa(even, odd).astype(BF16)
        for target, other, dims in ((node, node + 1, NT), (node + 1, node, NN)):
            couplings_v[target] = mm2(coeffs_v[other], near_k, dims)
    done += fetch(((couplings_v, couplings),), out_sems.at[pl.ds(2, 1)])
    for wait in done:
        wait()


def part(received, member, index):
    return received[member].astype(F32)[index * SHARE : (index + 1) * SHARE]


def level_sums(received, index):
    sums = [part(received, member, index) for member in range(MEMBERS)]
    for _ in range(index):
        sums = [sums[2 * n] + sums[2 * n + 1] for n in range(len(sums) // 2)]
    return sums


def total_kernel(received, send):
    total = level_sums(received, LEVELS)[0]
    total = jnp.concatenate([total, jnp.zeros_like(total)], axis=0).astype(BF16)
    for group in range(GROUPS):
        send[group] = total


def reply_kernel(received, totals, top_skel, reply):
    flat = jnp.concatenate([totals[group] for group in range(GROUPS)], axis=1)
    group = jnp.right_shift(lax.axis_index("pts"), LEVELS)
    (mine,) = extended(top_skel[group], True, False)
    mine = mine.T
    top_k = []
    for other in range(GROUPS):
        (theirs,) = extended(top_skel[other], False, True)
        value = jnp.exp2(mm(mine, theirs) * EXPO)
        top_k.append(jnp.where(group == other, 0.0, value).astype(BF16))
    field = mm(flat, jnp.concatenate(top_k, axis=1), NT)[:SHARE]
    levels = [level_sums(received, level) for level in range(LEVELS)]
    blank = jnp.zeros((SHARE, RANK), F32)
    for member in range(MEMBERS):
        rows = [levels[level][(member >> level) ^ 1] for level in range(LEVELS)]
        reply[member] = jnp.concatenate(rows + [field, blank], axis=0).astype(BF16)


def down_kernel(
    replies, chain_k, transfer, couplings, both, fields, give, keep
):
    core = lax.axis_index("rhs")
    table = replies[...].astype(F32)
    got = [
        table[:, index * SHARE : (index + 1) * SHARE].reshape(RANK, RANK)
        for index in range(LEVELS + 1)
    ]
    rows = jnp.concatenate([part.astype(BF16) for part in got], axis=1)
    field = mm(rows, chain_k[...].reshape((LEVELS + 1) * RANK, RANK))
    now = [field]
    for start, count, offset in ((6, 1, 12), (4, 2, 8), (0, 4, 0)):
        below = []
        for node in range(count):
            spread = mm2(now[node], transfer[start + node], NT)
            for child in range(2):
                rows = spread[:, child * RANK : (child + 1) * RANK]
                below.append(couplings[offset + 2 * node + child] + rows)
        now = below
    away = pl.multiple_of((1 - core) * RANK, RANK)
    stay = pl.multiple_of(core * RANK, RANK)
    for leaf in range(LEAVES):
        swapped = jnp.concatenate([now[leaf][DIM:], now[leaf][:DIM]], axis=0)
        terms = jnp.concatenate(split(swapped), axis=0)
        for target, first in ((give, away), (keep, stay)):
            rows = both[leaf, pl.ds(first, RANK), :]
            target[leaf] = mm(jnp.concatenate([rows, rows], axis=1), terms).astype(target.dtype)
    for leaf in range(LEAVES):
        fields[leaf] = now[leaf][:DIM].astype(BF16)


def finish_kernel(fields, basis, near, output):
    for leaf in range(LEAVES):
        far = mm(fields[leaf], basis[leaf], NT)
        output[:, pl.ds(leaf * ROWS, ROWS)] = (near[leaf] + far).astype(BF16)


def near_kernel(
    ids,
    valid,
    swap_a,
    own,
    swap_b,
    after,
    near,
    ids_v,
    valid_v,
    swap_a_v,
    own_v,
    swap_b_v,
    left,
    right,
    values,
    near_v,
    sems,
    near_sems,
):
    waits = fetch(
        ((own, own_v), (swap_a, swap_a_v), (swap_b, swap_b_v), (ids, ids_v), (valid, valid_v)),
        sems,
    )
    lane = lanes(ROWS).astype(F32).astype(BF16)
    edge = jnp.full((), DIM, BF16)
    device = lax.axis_index("pts")
    odd = jnp.bitwise_and(device, 1)
    places = ((2 - 2 * odd) * LEAVES, LEAVES, 2 * odd * LEAVES)
    for wait, index, block in ((0, 1, own_v), (1, 0, swap_a_v), (2, 2, swap_b_v)):
        waits[wait]()
        for leaf in range(LEAVES):
            value = block[leaf]
            turned = value.T
            made = norm_rows(turned[DIM:], index == 1, True)
            spare = made[-1].astype(BF16).T
            spare = jnp.concatenate([spare, jnp.zeros((ROWS, 112), BF16)], axis=1)
            values[places[index] + leaf] = turned[:DIM]
            right[places[index] + leaf] = jnp.where(lane < edge, spare, value)
            if index == 1:
                blank = jnp.zeros((DIM - 16, ROWS), BF16)
                left[leaf] = jnp.concatenate(
                    [made[0].astype(BF16), blank, turned[DIM:]], axis=0
                )
    shift = (device - 1) * LEAVES
    waits[3]()
    waits[4]()

    def body(leaf, carry):
        mine = left[leaf]
        total = jnp.zeros((DIM, ROWS), F32)
        for start in range(0, SLOTS, 4):
            tiles, others = [], []
            for slot in range(start, start + 4):
                where = ids_v[leaf, slot] - shift
                used = jnp.full((1, ROWS), valid_v[leaf, slot], jnp.int32).astype(F32).astype(BF16)
                tiles.append(jnp.exp2(mm(right[where], mine) * EXPO).astype(BF16))
                others.append(values[where] * used)
            total = total + mm(jnp.concatenate(others, axis=1), jnp.concatenate(tiles, axis=0))
        near_v[leaf] = total
        pltpu.make_async_copy(near_v.at[leaf], near.at[leaf], near_sems.at[leaf]).start()
        return carry

    lax.fori_loop(0, LEAVES, body, 0)
    for leaf in range(LEAVES):
        pltpu.make_async_copy(near_v.at[leaf], near.at[leaf], near_sems.at[leaf]).wait()


def local(
    points,
    inputs,
    cotangent,
    order,
    near_ids,
    near_valid,
    leaf_basis,
    local_transfer,
    chain_transfer,
    leaf_skel,
    local_skel,
    chain_skel,
    top_skel,
):
    count = lax.axis_size("pts")
    block = (LEAVES, ROWS, 128)

    points, inputs, cot = points.T, inputs.T, cotangent.T
    leaf_skel, local_skel, chain_skel, top_skel = (
        jnp.swapaxes(skel, -1, -2) for skel in (leaf_skel, local_skel, chain_skel, top_skel)
    )
    order = order.reshape(2 * LEAVES, 128)
    joined, coeffs, send = call(
        rise_kernel,
        (
            sds(block, BF16),
            sds((14, RANK, RANK), F32),
            sds((MEMBERS, SLAB, RANK), BF16),
        ),
        [HBM] * 7,
        [
            pltpu.VMEM((2 * DIM, LEAVES * ROWS), BF16),
            pltpu.VMEM((2 * LEAVES, 128), jnp.int32),
            pltpu.VMEM((DIM, LEAVES * ROWS), BF16),
            pltpu.VMEM(block, BF16),
            pltpu.VMEM(local_transfer.shape, BF16),
            pltpu.VMEM(chain_transfer.shape, BF16),
            pltpu.VMEM(block, BF16),
            pltpu.VMEM((14, RANK, RANK), F32),
            pltpu.VMEM((4, ROWS, 256), BF16),
            pltpu.SemaphoreType.DMA((7,)),
            pltpu.SemaphoreType.DMA((LEAVES,)),
            pltpu.SemaphoreType.DMA((3,)),
        ],
        places=(HBM, HBM, VMEM),
    )(points, inputs, order, cot, leaf_basis, local_transfer, chain_transfer)

    groups = [[g * MEMBERS + i for i in range(MEMBERS)] for g in range(GROUPS)]
    across = [[g * MEMBERS + i for g in range(GROUPS)] for i in range(MEMBERS)]
    received = lax.all_to_all(send, "pts", 0, 0, axis_index_groups=groups, tiled=True)

    swaps = []
    for first in (0, 1):
        pairs = [(i, i + 1) for i in range(first, count - 1, 2)]
        swaps.append(lax.ppermute(joined, "pts", pairs + [(b, a) for a, b in pairs]))

    total = call(
        total_kernel, sds((GROUPS, 2 * SHARE, RANK), BF16), [VMEM], room=8
    )(received)
    totals = lax.all_to_all(total, "pts", 0, 0, axis_index_groups=across, tiled=True)

    tree = (14, RANK, RANK)
    square = (LEAVES, RANK, RANK)
    links = (LEVELS + 1, RANK, RANK)
    couplings, chain_k, both = call(
        couple_kernel,
        (sds(tree, F32), sds(links, BF16), sds(block, BF16)),
        [HBM] * 7 + [ANY],
        [
            pltpu.VMEM(tree, F32),
            pltpu.VMEM(block, BF16),
            pltpu.VMEM((DIM, LEAVES * ROWS), BF16),
            pltpu.VMEM(leaf_skel.shape, BF16),
            pltpu.VMEM(local_skel.shape, BF16),
            pltpu.VMEM(chain_skel.shape, BF16),
            pltpu.VMEM(chain_transfer.shape, BF16),
            pltpu.VMEM(tree, F32),
            pltpu.VMEM(links, BF16),
            pltpu.VMEM(block, BF16),
            pltpu.SemaphoreType.DMA((7,)),
            pltpu.SemaphoreType.DMA((3,)),
        ],
        cost=(2 * 10**9, 4 * 10**6, 10**6),
        places=(HBM,) * 3,
    )(coeffs, joined, cot, leaf_skel, local_skel, chain_skel, chain_transfer, total)

    reply = call(
        reply_kernel, sds((MEMBERS, SLAB, RANK), BF16), [VMEM] * 3, room=8
    )(received, totals, top_skel)
    replies = lax.all_to_all(reply, "pts", 0, 0, axis_index_groups=groups, tiled=True)

    near = call(
        near_kernel,
        sds((LEAVES, DIM, ROWS), F32),
        [HBM] * 5 + [ANY],
        [
            pltpu.SMEM((LEAVES, SLOTS), jnp.int32),
            pltpu.SMEM((LEAVES, SLOTS), jnp.int32),
            pltpu.VMEM(block, BF16),
            pltpu.VMEM(block, BF16),
            pltpu.VMEM(block, BF16),
            pltpu.VMEM((LEAVES, 128, ROWS), BF16),
            pltpu.VMEM((3 * LEAVES, ROWS, 128), BF16),
            pltpu.VMEM((3 * LEAVES, DIM, ROWS), BF16),
            pltpu.VMEM((LEAVES, DIM, ROWS), F32),
            pltpu.SemaphoreType.DMA((5,)),
            pltpu.SemaphoreType.DMA((LEAVES,)),
        ],
        cost=(5 * 10**10, 4 * 10**6, LEAVES * 800000),
        places=HBM,
        room=14,
    )(near_ids, near_valid, swaps[0], joined, swaps[1], reply)

    fields, give, keep = call(
        down_kernel,
        (sds((LEAVES, DIM, RANK), BF16), sds(square, BF16), sds(square, F32)),
        [VMEM] * 5,
        room=14,
    )(replies, chain_k, local_transfer, couplings, both)
    got = lax.ppermute(give, "rhs", [(0, 1), (1, 0)])
    output = call(
        finish_kernel,
        sds((DIM, LEAVES * ROWS), BF16),
        [VMEM] * 3,
        cost=(3 * 10**9, 2 * 10**6, 0),
        room=14,
    )(fields, leaf_basis, near)
    basis_grad = (keep + got.astype(F32)).astype(BF16)
    return output.T, basis_grad


def solution(mesh):
    placed = (
        P("pts", None),
        P("pts", "rhs"),
        P("pts", "rhs"),
        P("pts"),
        P("pts", None),
        P("pts", None),
        P("pts", None, None),
        P("pts", None, None),
        P("pts", None, None, None),
        P("pts", None, None),
        P("pts", None, None),
        P("pts", None, None, None, None),
        P(),
    )
    return jax.shard_map(
        local,
        mesh=mesh,
        in_specs=placed,
        out_specs=(P("pts", "rhs"), P("pts", "rhs", None)),
        check_vma=False,
    )
```

```python
import math

import jax
import jax.numpy as jnp
from jax import lax
from jax.experimental import pallas as pl
from jax.experimental.pallas import tpu as pltpu
from jax.sharding import PartitionSpec as P

F32 = jnp.float32
BF16 = jnp.bfloat16

LEVELS = 4
MEMBERS = 16
GROUPS = 16
SLAB = 48
SHARE = 8
LEAVES = 8
ROWS = 256
RANK = 128
DIM = 64
SLOTS = 12

VMEM = pl.BlockSpec(memory_space=pltpu.VMEM)
ANY = pl.BlockSpec(memory_space=pl.ANY)
HBM = pl.BlockSpec(memory_space=pltpu.HBM)
NN = (((1,), (0,)), ((), ()))
NT = (((1,), (1,)), ((), ()))


def mm(a, b, dims=NN):
    return lax.dot_general(a, b, dims, preferred_element_type=F32)


def split(a):
    high = a.astype(BF16)
    return high, (a - high.astype(F32)).astype(BF16)


def mm2(a, b, dims=NN):
    high, low = split(a)
    along = dims[0][1][0]
    return mm(jnp.concatenate([high, low], axis=1), jnp.concatenate([b, b], axis=along), dims)


def lanes(rows, width=128):
    return lax.broadcasted_iota(jnp.int32, (rows, width), 1)


def norm_rows(pts, left, right):
    wide = pts.astype(F32)
    half = -0.5 * jnp.sum(wide * wide, axis=0, keepdims=True)
    first = half.astype(BF16).astype(F32)
    rest = half - first
    second = rest.astype(BF16).astype(F32)
    third = rest - second
    row = lax.broadcasted_iota(jnp.int32, (16, pts.shape[1]), 0)
    out = []
    for want, low, ones in ((left, 0, 3), (right, 3, 0)):
        if not want:
            continue
        value = jnp.where((row >= ones) & (row < ones + 3), 1.0, 0.0)
        for offset, term in enumerate((first, second, third)):
            value = jnp.where(row == low + offset, term, value)
        out.append(value)
    return out


def extended(pts, left, right):
    blank = jnp.zeros((128 - DIM - 16, pts.shape[1]), BF16)
    return [
        jnp.concatenate([pts, rows.astype(BF16), blank], axis=0)
        for rows in norm_rows(pts, left, right)
    ]


EXPO = 4.0 / (DIM * math.log(2.0))


def kappa(left_pts, right_pts):
    (left,) = extended(left_pts, True, False)
    (right,) = extended(right_pts, False, True)
    return jnp.exp2(mm(left.T, right) * EXPO)


def call(kernel, outs, specs, scratch=(), cost=(0, 0, 0), places=None, room=60):
    return pl.pallas_call(
        kernel,
        out_shape=outs,
        in_specs=specs,
        out_specs=places or jax.tree.map(lambda _: VMEM, outs),
        scratch_shapes=list(scratch),
        compiler_params=pltpu.CompilerParams(vmem_limit_bytes=int(room * 2**20)),
        cost_estimate=pl.CostEstimate(
            flops=cost[0], bytes_accessed=cost[1], transcendentals=cost[2]
        ),
    )


def sds(shape, dtype):
    return jax.ShapeDtypeStruct(shape, dtype)


def fetch(pairs, sems):
    copies = [
        pltpu.make_async_copy(source, target, sems.at[index])
        for index, (source, target) in enumerate(pairs)
    ]
    for copy in copies:
        copy.start()
    return [copy.wait for copy in copies]


def chain_products(chain, device):
    product, products = None, []
    for level in range(LEVELS):
        bit = jnp.bitwise_and(jnp.right_shift(device, level), 1)
        half = chain[0, level, pl.ds(pl.multiple_of(bit * RANK, RANK), RANK), :]
        product = half if product is None else mm(product, half).astype(BF16)
        products.append(product)
    return products


def rise_kernel(
    points,
    inputs,
    order,
    cot,
    basis,
    transfer,
    chain,
    joined,
    coeffs,
    send,
    raw_v,
    order_v,
    cot_v,
    basis_v,
    transfer_v,
    chain_v,
    joined_v,
    coeffs_v,
    source_v,
    in_sems,
    joined_sems,
    coeff_sems,
):
    waits = fetch(
        (
            (points, raw_v.at[pl.ds(DIM, DIM)]),
            (inputs, raw_v.at[pl.ds(0, DIM)]),
            (order, order_v),
            (chain, chain_v),
            (cot, cot_v),
            (basis, basis_v),
            (transfer, transfer_v),
        ),
        in_sems,
    )
    device = lax.axis_index("pts")
    base = device * (LEAVES * ROWS)
    for wait in waits[:4]:
        wait()
    products = chain_products(chain_v, device)
    for index in range(4):
        low = raw_v[:, pl.ds(index * 512, ROWS)].T
        high = raw_v[:, pl.ds(index * 512 + ROWS, ROWS)].T
        source_v[index] = jnp.concatenate([low, high], axis=1)
    lane = lanes(ROWS, ROWS).astype(F32).astype(BF16)
    one, zero = jnp.ones((), BF16), jnp.zeros((), BF16)
    joined_copies = []
    for leaf in range(LEAVES):
        pieces = [order_v[pl.ds(2 * leaf + index, 1), :] - base for index in range(2)]
        row = jnp.concatenate(pieces, axis=1)
        low = jnp.bitwise_and(row, 255).astype(F32)
        high = jnp.right_shift(row, 8).astype(F32)
        low = jnp.broadcast_to(low, (128, ROWS)).T.astype(BF16)
        high = jnp.broadcast_to(high, (128, ROWS)).T
        hit = jnp.where(jnp.concatenate([low, low], axis=1) == lane, one, zero)
        value = jnp.zeros((ROWS, 128), F32)
        for index in range(4):
            found = mm(hit, source_v[index])
            value = jnp.where(high == 2.0 * index, found[:, :128], value)
            value = jnp.where(high == 2.0 * index + 1.0, found[:, 128:], value)
        joined_v[leaf] = value.astype(BF16)
        copy = pltpu.make_async_copy(joined_v.at[leaf], joined.at[leaf], joined_sems.at[leaf])
        copy.start()
        joined_copies.append(copy)
    for wait in waits[4:]:
        wait()
    now = []
    for leaf in range(LEAVES):
        theirs = cot_v[:, pl.ds(leaf * ROWS, ROWS)]
        pair = jnp.concatenate([joined_v[leaf].T[:DIM], theirs], axis=0)
        now.append(mm(pair, basis_v[leaf]))
    offset, done, level = 0, 0, 0
    coeff_copies = []
    while len(now) > 1:
        for node, value in enumerate(now):
            coeffs_v[done + node] = value
        span = pl.ds(done, len(now))
        copy = pltpu.make_async_copy(coeffs_v.at[span], coeffs.at[span], coeff_sems.at[level])
        copy.start()
        coeff_copies.append(copy)
        done += len(now)
        level += 1
        now = [
            mm2(jnp.concatenate([now[2 * n], now[2 * n + 1]], axis=1), transfer_v[offset + n])
            for n in range(len(now) // 2)
        ]
        offset += len(now)
    above = mm(now[0].astype(BF16), jnp.concatenate(products, axis=1))
    parts = [now[0]]
    parts += [above[:, level * RANK : (level + 1) * RANK] for level in range(LEVELS)]
    parts = [part.reshape(MEMBERS, SHARE, RANK) for part in parts]
    parts.append(jnp.zeros((MEMBERS, SLAB - 5 * SHARE, RANK), F32))
    send[...] = jnp.concatenate(parts, axis=1).astype(BF16)
    for copy in joined_copies + coeff_copies:
        copy.wait()


def couple_kernel(
    coeffs,
    joined,
    cot,
    leaf_skel,
    local_skel,
    chain_skel,
    chain,
    after,
    couplings,
    chain_k,
    both,
    coeffs_v,
    joined_v,
    cot_v,
    leaf_v,
    local_v,
    skel_v,
    chain_v,
    couplings_v,
    chain_k_v,
    both_v,
    sems,
    out_sems,
):
    waits = fetch(
        (
            (chain_skel, skel_v),
            (chain, chain_v),
            (leaf_skel, leaf_v),
            (local_skel, local_v),
            (coeffs, coeffs_v),
            (cot, cot_v),
            (joined, joined_v),
        ),
        sems,
    )
    device = lax.axis_index("pts")
    for wait in waits[:2]:
        wait()
    products = chain_products(chain_v, device)
    for level in range(LEVELS):
        bit = jnp.bitwise_and(jnp.right_shift(device, level), 1)
        value = kappa(skel_v[0, level, 1 - bit], skel_v[0, level, bit]).astype(BF16)
        if level > 0:
            value = mm(value, products[level - 1], NT).astype(BF16)
        chain_k_v[level] = value
    chain_k_v[LEVELS] = products[LEVELS - 1].T
    done = fetch(((chain_k_v, chain_k),), out_sems)
    for wait in waits[2:5]:
        wait()
    for node in range(0, 14, 2):
        if node < 8:
            even, odd = leaf_v[node], leaf_v[node + 1]
        else:
            even, odd = local_v[node - 8], local_v[node - 7]
        near_k = kappa(even, odd).astype(BF16)
        for target, other, dims in ((node, node + 1, NT), (node + 1, node, NN)):
            couplings_v[target] = mm2(coeffs_v[other], near_k, dims)
    done += fetch(((couplings_v, couplings),), out_sems.at[pl.ds(1, 1)])
    for wait in waits[5:]:
        wait()
    for leaf in range(LEAVES):
        theirs = cot_v[:, pl.ds(leaf * ROWS, ROWS)].T
        both_v[leaf] = jnp.concatenate([joined_v[leaf][:, :DIM], theirs], axis=1)
    done += fetch(((both_v, both),), out_sems.at[pl.ds(2, 1)])
    for wait in done:
        wait()


def part(received, member, index):
    return received[member].astype(F32)[index * SHARE : (index + 1) * SHARE]


def level_sums(received, index):
    sums = [part(received, member, index) for member in range(MEMBERS)]
    for _ in range(index):
        sums = [sums[2 * n] + sums[2 * n + 1] for n in range(len(sums) // 2)]
    return sums


def total_kernel(received, send):
    total = level_sums(received, LEVELS)[0]
    total = jnp.concatenate([total, jnp.zeros_like(total)], axis=0).astype(BF16)
    for group in range(GROUPS):
        send[group] = total


def reply_kernel(received, totals, top_skel, reply):
    flat = jnp.concatenate([totals[group] for group in range(GROUPS)], axis=1)
    group = jnp.right_shift(lax.axis_index("pts"), LEVELS)
    (mine,) = extended(top_skel[group], True, False)
    mine = mine.T
    top_k = []
    for other in range(GROUPS):
        (theirs,) = extended(top_skel[other], False, True)
        value = jnp.exp2(mm(mine, theirs) * EXPO)
        top_k.append(jnp.where(group == other, 0.0, value).astype(BF16))
    field = mm(flat, jnp.concatenate(top_k, axis=1), NT)[:SHARE]
    levels = [level_sums(received, level) for level in range(LEVELS)]
    blank = jnp.zeros((SHARE, RANK), F32)
    for member in range(MEMBERS):
        rows = [levels[level][(member >> level) ^ 1] for level in range(LEVELS)]
        reply[member] = jnp.concatenate(rows + [field, blank], axis=0).astype(BF16)


def down_kernel(
    replies, chain_k, transfer, couplings, both, fields, give, keep
):
    core = lax.axis_index("rhs")
    table = replies[...].astype(F32)
    got = [
        table[:, index * SHARE : (index + 1) * SHARE].reshape(RANK, RANK)
        for index in range(LEVELS + 1)
    ]
    rows = jnp.concatenate([part.astype(BF16) for part in got], axis=1)
    field = mm(rows, chain_k[...].reshape((LEVELS + 1) * RANK, RANK))
    now = [field]
    for start, count, offset in ((6, 1, 12), (4, 2, 8), (0, 4, 0)):
        below = []
        for node in range(count):
            spread = mm2(now[node], transfer[start + node], NT)
            for child in range(2):
                rows = spread[:, child * RANK : (child + 1) * RANK]
                below.append(couplings[offset + 2 * node + child] + rows)
        now = below
    away = pl.multiple_of((1 - core) * RANK, RANK)
    stay = pl.multiple_of(core * RANK, RANK)
    for leaf in range(LEAVES):
        swapped = jnp.concatenate([now[leaf][DIM:], now[leaf][:DIM]], axis=0)
        terms = jnp.concatenate(split(swapped), axis=0)
        for target, first in ((give, away), (keep, stay)):
            rows = both[leaf, pl.ds(first, RANK), :]
            target[leaf] = mm(jnp.concatenate([rows, rows], axis=1), terms).astype(target.dtype)
    for leaf in range(LEAVES):
        fields[leaf] = now[leaf][:DIM].astype(BF16)


def finish_kernel(fields, basis, near, output):
    for leaf in range(LEAVES):
        far = mm(fields[leaf], basis[leaf], NT)
        output[:, pl.ds(leaf * ROWS, ROWS)] = (near[leaf] + far).astype(BF16)


def near_kernel(
    ids,
    valid,
    swap_a,
    own,
    swap_b,
    after,
    near,
    ids_v,
    valid_v,
    swap_a_v,
    own_v,
    swap_b_v,
    left,
    right,
    values,
    near_v,
    sems,
    near_sems,
):
    waits = fetch(
        ((own, own_v), (swap_a, swap_a_v), (swap_b, swap_b_v), (ids, ids_v), (valid, valid_v)),
        sems,
    )
    lane = lanes(ROWS).astype(F32).astype(BF16)
    edge = jnp.full((), DIM, BF16)
    device = lax.axis_index("pts")
    odd = jnp.bitwise_and(device, 1)
    places = ((2 - 2 * odd) * LEAVES, LEAVES, 2 * odd * LEAVES)
    for wait, index, block in ((0, 1, own_v), (1, 0, swap_a_v), (2, 2, swap_b_v)):
        waits[wait]()
        for leaf in range(LEAVES):
            value = block[leaf]
            turned = value.T
            made = norm_rows(turned[DIM:], index == 1, True)
            spare = made[-1].astype(BF16).T
            spare = jnp.concatenate([spare, jnp.zeros((ROWS, 112), BF16)], axis=1)
            values[places[index] + leaf] = turned[:DIM]
            right[places[index] + leaf] = jnp.where(lane < edge, spare, value)
            if index == 1:
                blank = jnp.zeros((DIM - 16, ROWS), BF16)
                left[leaf] = jnp.concatenate(
                    [made[0].astype(BF16), blank, turned[DIM:]], axis=0
                )
    shift = (device - 1) * LEAVES
    waits[3]()
    waits[4]()

    def body(leaf, carry):
        mine = left[leaf]
        total = jnp.zeros((DIM, ROWS), F32)
        for start in range(0, SLOTS, 4):
            tiles, others = [], []
            for slot in range(start, start + 4):
                where = ids_v[leaf, slot] - shift
                used = jnp.full((1, ROWS), valid_v[leaf, slot], jnp.int32).astype(F32).astype(BF16)
                tiles.append(jnp.exp2(mm(right[where], mine) * EXPO).astype(BF16))
                others.append(values[where] * used)
            total = total + mm(jnp.concatenate(others, axis=1), jnp.concatenate(tiles, axis=0))
        near_v[leaf] = total
        pltpu.make_async_copy(near_v.at[leaf], near.at[leaf], near_sems.at[leaf]).start()
        return carry

    lax.fori_loop(0, LEAVES, body, 0)
    for leaf in range(LEAVES):
        pltpu.make_async_copy(near_v.at[leaf], near.at[leaf], near_sems.at[leaf]).wait()


def local(
    points,
    inputs,
    cotangent,
    order,
    near_ids,
    near_valid,
    leaf_basis,
    local_transfer,
    chain_transfer,
    leaf_skel,
    local_skel,
    chain_skel,
    top_skel,
):
    count = lax.axis_size("pts")
    block = (LEAVES, ROWS, 128)

    points, inputs, cot = points.T, inputs.T, cotangent.T
    leaf_skel, local_skel, chain_skel, top_skel = (
        jnp.swapaxes(skel, -1, -2) for skel in (leaf_skel, local_skel, chain_skel, top_skel)
    )
    order = order.reshape(2 * LEAVES, 128)
    joined, coeffs, send = call(
        rise_kernel,
        (
            sds(block, BF16),
            sds((14, RANK, RANK), F32),
            sds((MEMBERS, SLAB, RANK), BF16),
        ),
        [HBM] * 7,
        [
            pltpu.VMEM((2 * DIM, LEAVES * ROWS), BF16),
            pltpu.VMEM((2 * LEAVES, 128), jnp.int32),
            pltpu.VMEM((DIM, LEAVES * ROWS), BF16),
            pltpu.VMEM(block, BF16),
            pltpu.VMEM(local_transfer.shape, BF16),
            pltpu.VMEM(chain_transfer.shape, BF16),
            pltpu.VMEM(block, BF16),
            pltpu.VMEM((14, RANK, RANK), F32),
            pltpu.VMEM((4, ROWS, 256), BF16),
            pltpu.SemaphoreType.DMA((7,)),
            pltpu.SemaphoreType.DMA((LEAVES,)),
            pltpu.SemaphoreType.DMA((3,)),
        ],
        places=(HBM, HBM, VMEM),
    )(points, inputs, order, cot, leaf_basis, local_transfer, chain_transfer)

    groups = [[g * MEMBERS + i for i in range(MEMBERS)] for g in range(GROUPS)]
    across = [[g * MEMBERS + i for g in range(GROUPS)] for i in range(MEMBERS)]
    received = lax.all_to_all(send, "pts", 0, 0, axis_index_groups=groups, tiled=True)

    swaps = []
    for first in (0, 1):
        pairs = [(i, i + 1) for i in range(first, count - 1, 2)]
        swaps.append(lax.ppermute(joined, "pts", pairs + [(b, a) for a, b in pairs]))

    total = call(
        total_kernel, sds((GROUPS, 2 * SHARE, RANK), BF16), [VMEM], room=8
    )(received)
    totals = lax.all_to_all(total, "pts", 0, 0, axis_index_groups=across, tiled=True)

    tree = (14, RANK, RANK)
    square = (LEAVES, RANK, RANK)
    links = (LEVELS + 1, RANK, RANK)
    couplings, chain_k, both = call(
        couple_kernel,
        (sds(tree, F32), sds(links, BF16), sds(block, BF16)),
        [HBM] * 7 + [ANY],
        [
            pltpu.VMEM(tree, F32),
            pltpu.VMEM(block, BF16),
            pltpu.VMEM((DIM, LEAVES * ROWS), BF16),
            pltpu.VMEM(leaf_skel.shape, BF16),
            pltpu.VMEM(local_skel.shape, BF16),
            pltpu.VMEM(chain_skel.shape, BF16),
            pltpu.VMEM(chain_transfer.shape, BF16),
            pltpu.VMEM(tree, F32),
            pltpu.VMEM(links, BF16),
            pltpu.VMEM(block, BF16),
            pltpu.SemaphoreType.DMA((7,)),
            pltpu.SemaphoreType.DMA((3,)),
        ],
        cost=(2 * 10**9, 4 * 10**6, 10**6),
        places=(HBM,) * 3,
    )(coeffs, joined, cot, leaf_skel, local_skel, chain_skel, chain_transfer, total)

    reply = call(
        reply_kernel, sds((MEMBERS, SLAB, RANK), BF16), [VMEM] * 3, room=8
    )(received, totals, top_skel)
    replies = lax.all_to_all(reply, "pts", 0, 0, axis_index_groups=groups, tiled=True)

    near = call(
        near_kernel,
        sds((LEAVES, DIM, ROWS), F32),
        [HBM] * 5 + [ANY],
        [
            pltpu.SMEM((LEAVES, SLOTS), jnp.int32),
            pltpu.SMEM((LEAVES, SLOTS), jnp.int32),
            pltpu.VMEM(block, BF16),
            pltpu.VMEM(block, BF16),
            pltpu.VMEM(block, BF16),
            pltpu.VMEM((LEAVES, 128, ROWS), BF16),
            pltpu.VMEM((3 * LEAVES, ROWS, 128), BF16),
            pltpu.VMEM((3 * LEAVES, DIM, ROWS), BF16),
            pltpu.VMEM((LEAVES, DIM, ROWS), F32),
            pltpu.SemaphoreType.DMA((5,)),
            pltpu.SemaphoreType.DMA((LEAVES,)),
        ],
        cost=(5 * 10**10, 4 * 10**6, LEAVES * 800000),
        places=HBM,
        room=14,
    )(near_ids, near_valid, swaps[0], joined, swaps[1], reply)

    fields, give, keep = call(
        down_kernel,
        (sds((LEAVES, DIM, RANK), BF16), sds(square, BF16), sds(square, F32)),
        [VMEM] * 5,
        room=14,
    )(replies, chain_k, local_transfer, couplings, both)
    got = lax.ppermute(give, "rhs", [(0, 1), (1, 0)])
    output = call(
        finish_kernel,
        sds((DIM, LEAVES * ROWS), BF16),
        [VMEM] * 3,
        cost=(3 * 10**9, 2 * 10**6, 0),
        room=14,
    )(fields, leaf_basis, near)
    basis_grad = (keep + got.astype(F32)).astype(BF16)
    return output.T, basis_grad


def solution(mesh):
    placed = (
        P("pts", None),
        P("pts", "rhs"),
        P("pts", "rhs"),
        P("pts"),
        P("pts", None),
        P("pts", None),
        P("pts", None, None),
        P("pts", None, None),
        P("pts", None, None, None),
        P("pts", None, None),
        P("pts", None, None),
        P("pts", None, None, None, None),
        P(),
    )
    return jax.shard_map(
        local,
        mesh=mesh,
        in_specs=placed,
        out_specs=(P("pts", "rhs"), P("pts", "rhs", None)),
        check_vma=False,
    )
```
